32 devices in a mesh: grp: 2 (over y), ctx: 4 (over z), head: 2 (over x), sub: 2 (over core).
Axes of the slice: x: 2, y: 2, z: 4, core: 2. Of those that a mesh axis runs over, the one named last changes fastest.
Arguments:
- queries: bfloat16 [1024, 8192], P(('grp', 'ctx'), 'head'), parts along dimension 0, may hold values from -120 to 120
- stretch_keys: bfloat16 [1024, 1024], P(('grp', 'ctx', 'sub'), 'head'), parts along dimension 0, may hold values from -6 to 6
- stretch_values: bfloat16 [1024, 1024], P(('grp', 'ctx', 'sub'), 'head'), parts along dimension 0, may hold values from -6 to 6
- cache_keys: bfloat16 [3072, 1024], P(('grp', 'ctx', 'sub'), 'head'), parts along dimension 0, may hold values from -6 to 6
- cache_values: bfloat16 [3072, 1024], P(('grp', 'ctx', 'sub'), 'head'), parts along dimension 0, may hold values from -6 to 6
- doc_lengths: int32 [24], P('grp'), parts along dimension 0, may hold values from 1 to 256, 2048 in all
Outputs:
- attended: bfloat16 [1024, 8192], P(('grp', 'ctx'), ('head', 'sub')), parts along dimension 0
The draws below stay inside these ranges and needn't reach their ends.
There are 2 independent parts, one for each index of `grp`. The reference program is written for one: setup_inputs(seed, part) draws one part's arguments, and reference() takes and returns one part's arrays. A program takes and returns all parts, laid end to end along the dimension named above; each array names one. Nothing has to cross between parts.
Inputs may be any that keep to these rules, and one draw needn't show every extreme that they name: `doc_lengths`: the 12 documents fill all 2048 positions in order, none longer than 256 tokens and one exactly 256.
All inputs are finite; a program needn't handle non-finite values.
Results may differ from the reference program's by a relative error of at most 0.013.
Values may be sent and summed in bfloat16 or wider, within the bound.
No kernel may reach another device: no remote copies, remote signals or barrier semaphores. Data moves between devices by JAX's collectives and lax.ppermute only.
A program may use at most 64 MiB of HBM per device.

```python
import math
import jax
import jax.numpy as jnp
import numpy as np
from jax import lax

Q_HEADS = 64
KV_HEADS = 8
HEAD_DIM = 128
NDOC = 12
STRETCH = 512
PREFIX = 1536
DOCMAX = 256


def key_base(key):
    return jnp.clip(jax.random.normal(jax.random.fold_in(key, 7101), (STRETCH, KV_HEADS * HEAD_DIM), jnp.float32), -4.5, 4.5)


def draw_stretch_keys(key, part):
    base = key_base(key)
    return base.astype(jnp.bfloat16)


def draw_queries(key, part):
    values = jnp.clip(jax.random.normal(jax.random.fold_in(key, 7103), (STRETCH, Q_HEADS * HEAD_DIM), jnp.float32), -4.5, 4.5)
    return values.astype(jnp.bfloat16)


def level_of(stream_key, dims, pieces, low, largest):
    loudness, own = 1.0, jax.random.fold_in(stream_key, 6)
    for axis_at, shards_of in pieces:
        heights = jnp.exp(jax.random.uniform(jax.random.fold_in(own, axis_at), (shards_of,), jnp.float32, low / len(pieces), largest / len(pieces)))
        loudness = loudness * jnp.repeat(heights, dims[axis_at] // shards_of).reshape([-1 if axis == axis_at else 1 for axis in range(len(dims))])
    return loudness


def length_profile(number_of, total, most, skew):
    loads = [(1 << 20) // math.isqrt(standing ** skew) + 1 for standing in range(2, number_of + 1)]
    spare, holding = total - most - (number_of - 1), [1] * (number_of - 1)
    while spare > 0:
        candidates = [i for i in range(number_of - 1) if holding[i] < most]
        pool, left = sum([loads[i] for i in candidates]), spare
        for i in candidates:
            more = min(most - holding[i], max(1, left * loads[i] // pool), spare)
            holding[i] = holding[i] + more
            spare = spare - more
    return np.array([most] + holding)


def uneven_parts(stream_key, count, total, reach, slope):
    if count == 2:
        one = jax.random.randint(stream_key, (), max(1, total - reach), min(reach, total - 1) + 1)
        return jnp.stack([one, total - one])
    lengths = jnp.asarray(length_profile(count, total, reach, slope), jnp.int32)
    twos = (count - 1) // 2
    source_of, sink = lengths[1:1 + 2 * twos:2], lengths[2:2 + 2 * twos:2]
    slack = jnp.minimum(source_of - 1, reach - sink)
    shifted = jax.random.randint(jax.random.fold_in(stream_key, 1), (twos,), 0, 1 << 20) % (slack + 1)
    lengths = lengths.at[1:1 + 2 * twos:2].set(source_of - shifted).at[2:2 + 2 * twos:2].set(sink + shifted)
    return lengths[jax.random.permutation(jax.random.fold_in(stream_key, 2), count)]


def bell_draw(own_key, shape, scale, limit, split=(), kind=jnp.bfloat16):
    entries = scale * jax.random.normal(own_key, shape, jnp.float32)
    if split:
        entries = entries * level_of(own_key, shape, split, -0.22, 0.18)
    return jnp.clip(entries, -limit, limit).astype(kind)


def setup_inputs(seed: int = 0, part: int = 0) -> dict:
    seeds = jax.random.split(jax.random.key(seed), 7)
    own_keys = jax.random.split(jax.random.fold_in(seeds[6], part), 7)
    queries = draw_queries(jax.random.fold_in(jax.random.fold_in(seeds[6], part), 71), part)
    stretch_keys = draw_stretch_keys(jax.random.fold_in(jax.random.fold_in(seeds[6], part), 71), part)
    stretch_values = bell_draw(own_keys[2], (STRETCH, KV_HEADS * HEAD_DIM), 1.0, 6.0, ((0, 8), (1, 2)))
    cache_keys = bell_draw(own_keys[3], (PREFIX, KV_HEADS * HEAD_DIM), 1.0, 6.0, ((0, 8), (1, 2)))
    cache_values = bell_draw(own_keys[4], (PREFIX, KV_HEADS * HEAD_DIM), 1.0, 6.0, ((0, 8), (1, 2)))
    doc_lengths = uneven_parts(own_keys[5], NDOC, PREFIX + STRETCH, DOCMAX, 2).astype(jnp.int32)
    return {"queries": queries, "stretch_keys": stretch_keys, "stretch_values": stretch_values, "cache_keys": cache_keys, "cache_values": cache_values, "doc_lengths": doc_lengths}


NEG_FILL = -1.0e30


def reference(queries, stretch_keys, stretch_values, cache_keys, cache_values, doc_lengths):
    prefix_len = cache_keys.shape[0]
    stretch_len = stretch_keys.shape[0]
    keys_all = jnp.concatenate([cache_keys, stretch_keys], axis=0)
    values_all = jnp.concatenate([cache_values, stretch_values], axis=0)
    doc_ends = jnp.cumsum(doc_lengths).astype(jnp.int32)
    positions = jnp.arange(prefix_len + stretch_len, dtype=jnp.int32)
    doc_index = jnp.sum((positions[:, None] >= doc_ends[None, :]).astype(jnp.int32), axis=1).astype(jnp.int32)
    group_size = Q_HEADS // KV_HEADS
    query_block = math.gcd(stretch_len, 512)
    window = DOCMAX + query_block
    score_scale = HEAD_DIM ** -0.5

    def one_block(block_index):
        query_first = (block_index * query_block).astype(jnp.int32)
        query_start = (prefix_len + query_first).astype(jnp.int32)
        key_start = (query_start - DOCMAX).astype(jnp.int32)
        query_rows = lax.dynamic_slice_in_dim(queries, query_first, query_block, 0)
        key_rows = lax.dynamic_slice_in_dim(keys_all, key_start, window, 0)
        value_rows = lax.dynamic_slice_in_dim(values_all, key_start, window, 0)
        query_pos = query_start + jnp.arange(query_block, dtype=jnp.int32)
        key_pos = key_start + jnp.arange(window, dtype=jnp.int32)
        query_doc = lax.dynamic_slice_in_dim(doc_index, query_start, query_block, 0)
        key_doc = lax.dynamic_slice_in_dim(doc_index, key_start, window, 0)
        allowed = (key_doc[None, :] == query_doc[:, None]) & (key_pos[None, :] <= query_pos[:, None])
        query_heads = query_rows.astype(jnp.float32).reshape(query_block, KV_HEADS, group_size, HEAD_DIM)
        key_heads = key_rows.astype(jnp.float32).reshape(window, KV_HEADS, HEAD_DIM)
        value_heads = value_rows.astype(jnp.float32).reshape(window, KV_HEADS, HEAD_DIM)
        scores = jnp.einsum("tgjd,kgd->gjtk", query_heads, key_heads) * score_scale
        scores = jnp.where(allowed, scores, NEG_FILL)
        row_max = jnp.max(scores, axis=3, keepdims=True)
        weights = jnp.where(allowed, jnp.exp(scores - row_max), 0.0)
        row_sum = jnp.sum(weights, axis=3)
        rounded = lax.optimization_barrier(weights.astype(jnp.bfloat16))
        rounded = rounded.astype(jnp.float32)
        weighted = jnp.einsum("gjtk,kgd->tgjd", rounded, value_heads)
        normed = weighted / jnp.transpose(row_sum, (2, 0, 1))[..., None]
        return normed.reshape(query_block, Q_HEADS * HEAD_DIM).astype(jnp.bfloat16)

    outputs = lax.map(one_block, jnp.arange(stretch_len // query_block, dtype=jnp.int32))
    return outputs.reshape(stretch_len, Q_HEADS * HEAD_DIM)
```

```python
import functools
import math

import jax
import jax.numpy as jnp
from jax import lax
from jax.experimental import pallas as pl
from jax.experimental.pallas import tpu as pltpu
from jax.sharding import PartitionSpec as P

HEAD_DIM = 128
NEG_FILL = -1e30
SCORE_SCALE = HEAD_DIM ** (-0.5)
EXP2_SCALE = SCORE_SCALE * math.log2(math.e)
DOT_HEADS = 4


def ring(x, axis, steps):
    count = lax.axis_size(axis)
    return lax.ppermute(x, axis, [(i, (i + steps) % count) for i in range(count)])


def window_kernel(
    reach, picks, prefix_len, place_ref, lengths_ref, q_ref, own_ref, *refs
):
    ring_refs, extra_refs, o_ref = refs[:reach], refs[reach:-1], refs[-1]
    tok_rows, head_cols = q_ref.shape
    kv_cols = own_ref.shape[-1] // 2
    group_count = kv_cols // HEAD_DIM
    per_group = head_cols // kv_cols
    ctx_pos = place_ref[0]
    first = prefix_len + ctx_pos * tok_rows

    own = own_ref[...].reshape(tok_rows, 2 * kv_cols)
    blocks = [own]
    for distance in range(1, reach + 1):
        block = ring_refs[distance - 1][...]
        for extra, dest in picks[distance]:
            block = jnp.where(ctx_pos == dest, extra_refs[extra][...], block)
        blocks.append(block)

    row = lax.broadcasted_iota(jnp.int32, (tok_rows, tok_rows), 0)
    lane = lax.broadcasted_iota(jnp.int32, (tok_rows, tok_rows), 1)
    doc_start = jnp.zeros((tok_rows, tok_rows), jnp.int32)
    end = jnp.int32(0)
    for doc in range(lengths_ref.shape[0]):
        end = end + lengths_ref[doc]
        doc_start = jnp.where(first + row >= end, end, doc_start)
    allowed = [(first + lane >= doc_start) & (lane <= row)]
    for distance in range(1, reach + 1):
        allowed.append(first - distance * tok_rows + lane >= doc_start)
    allowed = jnp.concatenate(allowed, axis=1)
    keys_len = allowed.shape[1]
    ones = jnp.ones((keys_len, HEAD_DIM), jnp.bfloat16)

    for group in range(group_count):
        at = group * HEAD_DIM
        keys = jnp.concatenate([b[:, at : at + HEAD_DIM] for b in blocks], axis=0)
        at = at + kv_cols
        values = jnp.concatenate([b[:, at : at + HEAD_DIM] for b in blocks], axis=0)
        values = jnp.concatenate([values, ones], axis=1)
        for head in range(group * per_group, (group + 1) * per_group):
            here = pl.ds(head * HEAD_DIM, HEAD_DIM)
            scores = lax.dot_general(
                q_ref[:, here],
                keys,
                (((1,), (1,)), ((), ())),
                preferred_element_type=jnp.float32,
            )
            scores = jnp.where(allowed, scores, NEG_FILL)
            row_max = jnp.max(scores, axis=1, keepdims=True)
            rounded = jnp.exp2((scores - row_max) * EXP2_SCALE).astype(jnp.bfloat16)
            summed = jnp.dot(rounded, values, preferred_element_type=jnp.float32)
            o_ref[:, here] = (summed[:, :HEAD_DIM] / summed[:, HEAD_DIM:]).astype(o_ref.dtype)


def plan_extras(n_ctx, reach, per_shard):
    rounds = []
    for back in range(2, reach + 1):
        source = n_ctx - 1 - (back - 1) // per_shard
        block = per_shard - 1 - (back - 1) % per_shard
        for dest in range(reach + 1 - back):
            for step in rounds:
                if source not in step and all(d != dest for _, d, _ in step.values()):
                    break
            else:
                step = {}
                rounds.append(step)
            step[source] = (block, dest, dest + back)
    return rounds


def on_device(queries, stretch_keys, stretch_values, cache_keys, cache_values, doc_lengths):
    n_ctx = lax.axis_size("ctx")
    n_sub = lax.axis_size("sub")
    ctx_pos = lax.axis_index("ctx")
    sub_pos = lax.axis_index("sub")
    tok_rows = queries.shape[0]
    stretch_part = stretch_keys.shape[0]
    cache_part = cache_keys.shape[0]
    prefix_len = cache_part * n_sub * n_ctx
    group_count = stretch_keys.shape[1] // HEAD_DIM
    head_cols = queries.shape[1] // n_sub
    reach = n_ctx // 2
    per_shard = cache_part * n_sub // tok_rows

    keys = jnp.concatenate([stretch_keys, cache_keys], axis=0)
    values = jnp.concatenate([stretch_values, cache_values], axis=0)
    if group_count % n_sub == 0:
        kv_cols = stretch_keys.shape[1] // n_sub

        def share(which):
            at = which * kv_cols
            return jnp.concatenate(
                [
                    lax.dynamic_slice_in_dim(keys, at, kv_cols, 1),
                    lax.dynamic_slice_in_dim(values, at, kv_cols, 1),
                ],
                axis=1,
            )

        mine = share(sub_pos)
        theirs = share(1 - sub_pos)
    else:
        mine = theirs = jnp.concatenate([keys, values], axis=1)
    peers = lax.ppermute(theirs, "sub", [(0, 1), (1, 0)])
    halves = jnp.where(sub_pos == 0, jnp.stack([mine, peers]), jnp.stack([peers, mine]))
    own = halves[:, :stretch_part].reshape(tok_rows, -1)
    cached = halves[:, stretch_part:].reshape(n_sub * cache_part, -1)

    def cached_block(block):
        return lax.dynamic_slice_in_dim(cached, block * tok_rows, tok_rows, 0)

    outgoing = jnp.where(ctx_pos == n_ctx - 1, cached_block(per_shard - 1), own)
    rings = [ring(outgoing, "ctx", distance) for distance in range(1, reach + 1)]
    extras, picks = [], [[] for _ in range(reach + 1)]
    for step in plan_extras(n_ctx, reach, per_shard):
        blocks = [step.get(source, (0,))[0] for source in range(n_ctx)]
        block = jnp.take(jnp.array(blocks, jnp.int32), ctx_pos)
        if len(step) == 1:
            block = max(blocks)
        pairs = [(source, dest) for source, (_, dest, _) in step.items()]
        for _, dest, slot in step.values():
            picks[slot].append((len(extras), dest))
        extras.append(lax.ppermute(cached_block(block), "ctx", pairs))

    mine_q = lax.dynamic_slice_in_dim(queries, sub_pos * head_cols, head_cols, 1)
    vmem = pl.BlockSpec(memory_space=pltpu.VMEM)
    smem = pl.BlockSpec(memory_space=pltpu.SMEM)
    return pl.pallas_call(
        functools.partial(window_kernel, reach, picks, prefix_len),
        out_shape=jax.ShapeDtypeStruct((tok_rows, head_cols), queries.dtype),
        in_specs=[smem, smem] + [vmem] * (2 + reach + len(extras)),
        out_specs=vmem,
        compiler_params=pltpu.CompilerParams(vmem_limit_bytes=24 << 20),
    )(ctx_pos[None], doc_lengths, mine_q, own, *rings, *extras)


def solution(mesh):
    in_specs = (
        P(("grp", "ctx"), "head"),
        P(("grp", "ctx", "sub"), "head"),
        P(("grp", "ctx", "sub"), "head"),
        P(("grp", "ctx", "sub"), "head"),
        P(("grp", "ctx", "sub"), "head"),
        P("grp"),
    )
    out_specs = P(("grp", "ctx"), ("head", "sub"))
    return jax.shard_map(
        on_device, mesh=mesh, in_specs=in_specs, out_specs=out_specs, check_vma=False
    )
```

```python
import functools
import math

import jax
import jax.numpy as jnp
from jax import lax
from jax.experimental import pallas as pl
from jax.experimental.pallas import tpu as pltpu
from jax.sharding import PartitionSpec as P

HEAD_DIM = 128
NEG_FILL = -1e30
SCORE_SCALE = HEAD_DIM ** (-0.5)
EXP2_SCALE = SCORE_SCALE * math.log2(math.e)


def ring(x, axis, steps):
    count = lax.axis_size(axis)
    return lax.ppermute(x, axis, [(i, (i + steps) % count) for i in range(count)])


def pack_kernel(tok_rows, n_ctx, prefix_len, k_ref, v_ref, ck_ref, cv_ref, len_ref,
                mine_ref, theirs_ref, branch_ref, bias_ref, lengths, sems, len_sem):
    sub_pos = lax.axis_index("sub")
    stretch_part, cache_part = k_ref.shape[0], ck_ref.shape[0]
    kv_cols = mine_ref.shape[1] // 2
    split = kv_cols != k_ref.shape[1]
    copies = [pltpu.make_async_copy(len_ref, lengths, len_sem)]
    for out, owner in enumerate([sub_pos, 1 - sub_pos]):
        dst = (mine_ref, theirs_ref)[out]
        at = pl.multiple_of(owner * kv_cols, HEAD_DIM) if split else 0
        for i, (src, row, rows, col) in enumerate([
            (k_ref, 0, stretch_part, 0),
            (v_ref, 0, stretch_part, kv_cols),
            (ck_ref, stretch_part, cache_part, 0),
            (cv_ref, stretch_part, cache_part, kv_cols),
        ]):
            copies.append(
                pltpu.make_async_copy(
                    src.at[:, pl.ds(at, kv_cols)],
                    dst.at[pl.ds(row, rows), pl.ds(col, kv_cols)],
                    sems.at[out, i],
                )
            )
    for copy in copies:
        copy.start()
    copies[0].wait()
    starts = [jnp.int32(0)] * n_ctx
    end = jnp.int32(0)
    for doc in range(lengths.shape[0]):
        end = end + lengths[doc]
        for c in range(n_ctx):
            starts[c] = jnp.where(end <= prefix_len + c * tok_rows, end, starts[c])
    beyond = [prefix_len + c * tok_rows - starts[c] > tok_rows for c in range(n_ctx)]
    any_beyond = functools.reduce(jnp.logical_or, beyond)
    branch_ref[0] = jnp.where(beyond[0], 2, jnp.where(any_beyond, 1, 0))
    write_bias(prefix_len + lax.axis_index("ctx") * tok_rows, lengths, bias_ref)
    for copy in copies[1:]:
        copy.wait()


def write_bias(first, lengths, bias_ref):
    tok_rows = bias_ref.shape[0]
    row = lax.broadcasted_iota(jnp.int32, (tok_rows, tok_rows), 0)
    lane = lax.broadcasted_iota(jnp.int32, (tok_rows, tok_rows), 1)
    doc_start = jnp.zeros((tok_rows, tok_rows), jnp.int32)
    end = jnp.int32(0)
    for doc in range(lengths.shape[0]):
        end = end + lengths[doc]
        doc_start = jnp.where(first + row >= end, end, doc_start)
    for distance in range(bias_ref.shape[1] // tok_rows):
        allowed = first - distance * tok_rows + lane >= doc_start
        if distance == 0:
            allowed = allowed & (lane <= row)
        bias_ref[:, distance * tok_rows : (distance + 1) * tok_rows] = jnp.where(
            allowed, 0.0, NEG_FILL
        )


def window_kernel(picks, q_ref, bias_ref, *refs):
    own_ref, before_ref, *later_refs, o_ref = refs
    ctx_pos = lax.axis_index("ctx")
    blocks = [own_ref[...], before_ref[...]] + [None] * (bias_ref.shape[1] // q_ref.shape[0] - 2)
    for later_ref, pick in zip(later_refs, picks):
        for slot in sorted({slot for _, slot in pick}):
            here = [ctx_pos == dest for dest, at in pick if at == slot]
            block = later_ref[...]
            if blocks[slot] is not None:
                block = jnp.where(functools.reduce(jnp.logical_or, here), block, blocks[slot])
            blocks[slot] = block
    kv_cols = own_ref.shape[-1] // 2
    group_count = kv_cols // HEAD_DIM
    per_group = q_ref.shape[1] // kv_cols
    ones = jnp.ones((bias_ref.shape[1], HEAD_DIM), jnp.bfloat16)
    for group in range(group_count):
        at = group * HEAD_DIM
        keys = jnp.concatenate([b[:, at : at + HEAD_DIM] for b in blocks], axis=0)
        at = at + kv_cols
        values = jnp.concatenate([b[:, at : at + HEAD_DIM] for b in blocks], axis=0)
        values = jnp.concatenate([values, ones], axis=1)
        for head in range(group * per_group, (group + 1) * per_group):
            here = pl.ds(head * HEAD_DIM, HEAD_DIM)
            scores = lax.dot_general(
                q_ref[:, here],
                keys,
                (((1,), (1,)), ((), ())),
                preferred_element_type=jnp.float32,
            )
            scores = scores + bias_ref[...]
            row_max = jnp.max(scores, axis=1, keepdims=True)
            rounded = jnp.exp2((scores - row_max) * EXP2_SCALE).astype(jnp.bfloat16)
            summed = jnp.dot(rounded, values, preferred_element_type=jnp.float32)
            o_ref[:, here] = (summed[:, :HEAD_DIM] / summed[:, HEAD_DIM:]).astype(o_ref.dtype)


def plan_rounds(n_ctx, reach, per_shard):
    wanted = []
    for dest in range(n_ctx):
        for slot in range(2, reach + 1):
            back = slot - dest
            if back <= 0:
                wanted.append((dest - slot, 0, dest, slot))
            else:
                source = n_ctx - 1 - (back - 1) // per_shard
                wanted.append((source, per_shard - (back - 1) % per_shard, dest, slot))
    rounds = []
    for source, block, dest, slot in wanted:
        for step in rounds:
            if source not in step and all(d != dest for _, d, _ in step.values()):
                break
        else:
            step = {}
            rounds.append(step)
        step[source] = (block, dest, slot)
    return rounds


def on_device(queries, stretch_keys, stretch_values, cache_keys, cache_values, doc_lengths):
    n_ctx = lax.axis_size("ctx")
    n_sub = lax.axis_size("sub")
    ctx_pos = lax.axis_index("ctx")
    sub_pos = lax.axis_index("sub")
    tok_rows = queries.shape[0]
    stretch_part = stretch_keys.shape[0]
    cache_part = cache_keys.shape[0]
    part_rows = stretch_part + cache_part
    prefix_len = cache_part * n_sub * n_ctx
    group_count = stretch_keys.shape[1] // HEAD_DIM
    head_cols = queries.shape[1] // n_sub
    reach = n_ctx // 2
    per_shard = cache_part * n_sub // tok_rows
    kv_cols = stretch_keys.shape[1]
    if group_count % n_sub == 0:
        kv_cols = kv_cols // n_sub
    vmem = pl.BlockSpec(memory_space=pltpu.VMEM)
    smem = pl.BlockSpec(memory_space=pltpu.SMEM)
    hbm = pl.BlockSpec(memory_space=pltpu.HBM)

    half = jax.ShapeDtypeStruct((part_rows, 2 * kv_cols), stretch_keys.dtype)
    allowed = jax.ShapeDtypeStruct((tok_rows, (reach + 1) * tok_rows), jnp.float32)
    mine, theirs, branch, bias = pl.pallas_call(
        functools.partial(pack_kernel, tok_rows, n_ctx, prefix_len),
        out_shape=[half, half, jax.ShapeDtypeStruct((1,), jnp.int32), allowed],
        in_specs=[hbm] * 5,
        out_specs=[vmem, vmem, smem, vmem],
        scratch_shapes=[
            pltpu.SMEM(doc_lengths.shape, jnp.int32),
            pltpu.SemaphoreType.DMA((2, 4)),
            pltpu.SemaphoreType.DMA,
        ],
        compiler_params=pltpu.CompilerParams(vmem_limit_bytes=8 << 20),
    )(
        *[
            pltpu.with_memory_space_constraint(x, pltpu.HBM)
            for x in (stretch_keys, stretch_values, cache_keys, cache_values, doc_lengths)
        ]
    )
    peers = lax.ppermute(theirs, "sub", [(0, 1), (1, 0)])
    halves = jnp.where(sub_pos == 0, jnp.stack([mine, peers]), jnp.stack([peers, mine]))
    blocks = jnp.concatenate(
        [
            halves[:, :stretch_part].reshape(tok_rows, -1),
            halves[:, stretch_part:].reshape(n_sub * cache_part, -1),
        ]
    )
    own = blocks[:tok_rows]

    def block_at(index):
        return lax.dynamic_slice_in_dim(blocks, index * tok_rows, tok_rows, 0)

    outgoing = block_at(jnp.where(ctx_pos == n_ctx - 1, per_shard, 0))
    later, picks = [], []
    for step in plan_rounds(n_ctx, reach, per_shard):
        which = max(block for block, _, _ in step.values())
        for source, (block, _, _) in step.items():
            which = jnp.where(ctx_pos == source, block, which)
        pairs = [(source, dest) for source, (_, dest, _) in step.items()]
        later.append(lax.ppermute(block_at(which), "ctx", pairs))
        picks.append([(dest, slot) for _, dest, slot in step.values()])
    before = ring(outgoing, "ctx", 1)

    mine_q = lax.dynamic_slice_in_dim(queries, sub_pos * head_cols, head_cols, 1)
    return pl.pallas_call(
        functools.partial(window_kernel, picks),
        out_shape=jax.ShapeDtypeStruct((tok_rows, head_cols), queries.dtype),
        in_specs=[vmem] * (4 + len(later)),
        out_specs=vmem,
        compiler_params=pltpu.CompilerParams(vmem_limit_bytes=24 << 20),
    )(mine_q, bias, own, before, *later)


def solution(mesh):
    in_specs = (
        P(("grp", "ctx"), "head"),
        P(("grp", "ctx", "sub"), "head"),
        P(("grp", "ctx", "sub"), "head"),
        P(("grp", "ctx", "sub"), "head"),
        P(("grp", "ctx", "sub"), "head"),
        P("grp"),
    )
    out_specs = P(("grp", "ctx"), ("head", "sub"))
    return jax.shard_map(
        on_device, mesh=mesh, in_specs=in_specs, out_specs=out_specs, check_vma=False
    )
```

```python
import functools
import math

import jax
import jax.numpy as jnp
from jax import lax
from jax.experimental import pallas as pl
from jax.experimental.pallas import tpu as pltpu
from jax.sharding import PartitionSpec as P

HEAD_DIM = 128
NEG_FILL = -1e30
SCORE_SCALE = HEAD_DIM ** (-0.5)
EXP2_SCALE = SCORE_SCALE * math.log2(math.e)


def swap_cores(x):
    return lax.ppermute(x, "sub", [(0, 1), (1, 0)])


def pack_kernel(n_ctx, k_ref, v_ref, ck_ref, cv_ref, raw_ref, mine_ref, theirs_ref, sems):
    sub_pos = lax.axis_index("sub")
    last = lax.axis_index("ctx") == n_ctx - 1
    stretch_part, all_cols = k_ref.shape
    cache_part = ck_ref.shape[0]
    kv_cols = mine_ref.shape[1] // 2
    split = kv_cols != all_cols
    copies = []
    for i, (own_src, cache_src) in enumerate([(k_ref, ck_ref), (v_ref, cv_ref)]):
        dst = raw_ref.at[:, pl.ds(i * all_cols, all_cols)]
        from_own = pltpu.make_async_copy(own_src, dst, sems.at[0, i])
        tail = cache_src.at[pl.ds(cache_part - stretch_part, stretch_part), :]
        from_cache = pltpu.make_async_copy(tail, dst, sems.at[0, i])
        pl.when(last)(from_cache.start)
        pl.when(jnp.logical_not(last))(from_own.start)
        copies.append(from_own)
    for out, owner in ((2, 1 - sub_pos), (1, sub_pos)):
        dst = (None, mine_ref, theirs_ref)[out]
        at = pl.multiple_of(owner * kv_cols, HEAD_DIM) if split else 0
        for i, (src, row, rows, col) in enumerate([
            (k_ref, 0, stretch_part, 0),
            (v_ref, 0, stretch_part, kv_cols),
            (ck_ref, stretch_part, cache_part, 0),
            (cv_ref, stretch_part, cache_part, kv_cols),
        ]):
            copy = pltpu.make_async_copy(
                src.at[:, pl.ds(at, kv_cols)],
                dst.at[pl.ds(row, rows), pl.ds(col, kv_cols)],
                sems.at[out, i],
            )
            copy.start()
            copies.append(copy)
    for copy in copies:
        copy.wait()


def bias_kernel(prefix_len, stretch_part, cache_part, len_ref, bias_ref, lengths, sem):
    copy = pltpu.make_async_copy(len_ref, lengths, sem)
    copy.start()
    sub_pos, ctx_pos = lax.axis_index("sub"), lax.axis_index("ctx")
    tok_rows = bias_ref.shape[0]
    n_sub = tok_rows // stretch_part
    first = prefix_len + ctx_pos * tok_rows
    row = lax.broadcasted_iota(jnp.int32, (tok_rows, tok_rows), 0)
    lane = lax.broadcasted_iota(jnp.int32, (tok_rows, tok_rows), 1)
    doc_start = jnp.zeros((tok_rows, tok_rows), jnp.int32)
    copy.wait()
    end = jnp.int32(0)
    for doc in range(lengths.shape[0]):
        end = end + lengths[doc]
        doc_start = jnp.where(first + row >= end, end, doc_start)
    for slot in range(bias_ref.shape[1] // tok_rows):
        at = first - slot * tok_rows
        low, high = at + sub_pos * stretch_part, at + (1 - sub_pos) * stretch_part
        if slot == 1:
            tail = prefix_len - (n_sub - 1) * cache_part - stretch_part
            low = jnp.where(ctx_pos == 0, tail + sub_pos * cache_part, low)
            high = jnp.where(ctx_pos == 0, tail + (1 - sub_pos) * cache_part, high)
        elif slot > 1:
            at = jnp.where(ctx_pos == 0, prefix_len - cache_part, at) if slot == 2 else at
            low = jnp.where(ctx_pos < slot, at, low)
            high = jnp.where(ctx_pos < slot, at + stretch_part, high)
        key = jnp.where(lane < stretch_part, low + lane, high + lane - stretch_part)
        allowed = key >= doc_start
        if slot == 0:
            allowed = allowed & (key <= first + row)
        bias_ref[:, slot * tok_rows : (slot + 1) * tok_rows] = jnp.where(allowed, 0.0, NEG_FILL)


def window_kernel(picks, q_ref, bias_ref, own_ref, peer_ref, near_ref, far_ref, *refs):
    later_refs, o_ref = refs[:-1], refs[-1]
    ctx_pos = lax.axis_index("ctx")
    stretch_part, kv_cols = near_ref.shape[0], own_ref.shape[1] // 2
    own = own_ref[:stretch_part], peer_ref[:stretch_part]
    all_cols = near_ref.shape[1] // 2
    at = [0, all_cols]
    if all_cols != kv_cols:
        at = [pl.multiple_of(lax.axis_index("sub") * kv_cols + x, HEAD_DIM) for x in at]
    near = jnp.concatenate([near_ref[:, pl.ds(x, kv_cols)] for x in at], axis=1)
    blocks = [jnp.concatenate(own, axis=0), jnp.concatenate([near, far_ref[...]], axis=0)]
    blocks += [None] * (bias_ref.shape[1] // q_ref.shape[0] - 2)
    for later_ref, pick in zip(later_refs, picks):
        for slot in sorted({slot for _, slot in pick}):
            here = [ctx_pos == dest for dest, at in pick if at == slot]
            block = later_ref[...]
            if blocks[slot] is not None:
                block = jnp.where(functools.reduce(jnp.logical_or, here), block, blocks[slot])
            blocks[slot] = block
    group_count = kv_cols // HEAD_DIM
    per_group = q_ref.shape[1] // kv_cols
    ones = jnp.ones((bias_ref.shape[1], HEAD_DIM), jnp.bfloat16)
    for group in range(group_count):
        at = group * HEAD_DIM
        keys = jnp.concatenate([b[:, at : at + HEAD_DIM] for b in blocks], axis=0)
        at = at + kv_cols
        values = jnp.concatenate([b[:, at : at + HEAD_DIM] for b in blocks], axis=0)
        values = jnp.concatenate([values, ones], axis=1)
        for head in range(group * per_group, (group + 1) * per_group):
            here = pl.ds(head * HEAD_DIM, HEAD_DIM)
            scores = lax.dot_general(
                q_ref[:, here],
                keys,
                (((1,), (1,)), ((), ())),
                preferred_element_type=jnp.float32,
            )
            scores = scores + bias_ref[...]
            row_max = jnp.max(scores, axis=1, keepdims=True)
            rounded = jnp.exp2((scores - row_max) * EXP2_SCALE).astype(jnp.bfloat16)
            summed = jnp.dot(rounded, values, preferred_element_type=jnp.float32)
            o_ref[:, here] = (summed[:, :HEAD_DIM] / summed[:, HEAD_DIM:]).astype(o_ref.dtype)


def plan_rounds(n_ctx, reach, tok_rows, cache_part, shard_rows):
    per_shard = shard_rows // tok_rows
    cached, stretch = [], []
    for dest in range(n_ctx):
        for slot in range(2, reach + 1):
            back = slot - dest
            if back <= 0:
                stretch.append((dest - slot, None, dest, slot))
                continue
            source = n_ctx - 1 - (back - 1) // per_shard
            row = shard_rows - ((back - 1) % per_shard + 1) * tok_rows
            if dest == 0 and back == 2:
                row = cache_part
            cached.append((source, row, dest, slot))
    rounds = []
    for source, row, dest, slot in cached + stretch:
        dests = [{d for _, d, _ in step.values()} for step in rounds]
        free = [i for i, step in enumerate(rounds) if source not in step and dest not in dests[i]]
        free.sort(key=lambda i: source not in dests[i])
        if not free:
            rounds.append({})
            free = [len(rounds) - 1]
        rounds[free[0]][source] = (row, dest, slot)
    return rounds


def on_device(queries, stretch_keys, stretch_values, cache_keys, cache_values, doc_lengths):
    n_ctx = lax.axis_size("ctx")
    n_sub = lax.axis_size("sub")
    ctx_pos = lax.axis_index("ctx")
    sub_pos = lax.axis_index("sub")
    tok_rows = queries.shape[0]
    stretch_part, all_cols = stretch_keys.shape
    cache_part = cache_keys.shape[0]
    prefix_len = cache_part * n_sub * n_ctx
    head_cols = queries.shape[1] // n_sub
    reach = n_ctx // 2
    assert cache_part == 3 * stretch_part and tok_rows == 2 * stretch_part
    kv_cols = all_cols // n_sub if all_cols // HEAD_DIM % n_sub == 0 else all_cols
    vmem = pl.BlockSpec(memory_space=pltpu.VMEM)
    hbm = pl.BlockSpec(memory_space=pltpu.HBM)
    small = pltpu.CompilerParams(vmem_limit_bytes=8 << 20)

    def in_hbm(*arrays):
        return [pltpu.with_memory_space_constraint(x, pltpu.HBM) for x in arrays]

    half = jax.ShapeDtypeStruct((stretch_part + cache_part, 2 * kv_cols), stretch_keys.dtype)
    raw, mine, theirs = pl.pallas_call(
        functools.partial(pack_kernel, n_ctx),
        out_shape=[
            jax.ShapeDtypeStruct((stretch_part, 2 * all_cols), stretch_keys.dtype), half, half
        ],
        in_specs=[hbm] * 4,
        out_specs=[vmem] * 3,
        scratch_shapes=[pltpu.SemaphoreType.DMA((3, 4))],
        compiler_params=small,
    )(*in_hbm(stretch_keys, stretch_values, cache_keys, cache_values))
    bias = pl.pallas_call(
        functools.partial(bias_kernel, prefix_len, stretch_part, cache_part),
        out_shape=jax.ShapeDtypeStruct((tok_rows, (reach + 1) * tok_rows), jnp.float32),
        in_specs=[hbm],
        out_specs=vmem,
        scratch_shapes=[pltpu.SMEM(doc_lengths.shape, jnp.int32), pltpu.SemaphoreType.DMA],
        compiler_params=small,
    )(*in_hbm(doc_lengths))

    peers = swap_cores(theirs)
    near = lax.ppermute(raw, "ctx", [(i, (i + 1) % n_ctx) for i in range(n_ctx)])

    def cached_rows(row):
        parts = []
        for owner in range(n_sub):
            low = max(row, owner * cache_part) - owner * cache_part + stretch_part
            high = min(row + tok_rows, (owner + 1) * cache_part) - owner * cache_part + stretch_part
            if low < high:
                parts.append(jnp.where(sub_pos == owner, mine[low:high], peers[low:high]))
        return jnp.concatenate(parts) if len(parts) > 1 else parts[0]

    own = jnp.concatenate([mine[:stretch_part], peers[:stretch_part]])
    sent, later, picks = [], [], []
    for step in plan_rounds(n_ctx, reach, tok_rows, cache_part, cache_part * n_sub):
        block = own
        for source, (row, _, _) in step.items():
            if row is not None:
                block = jnp.where(ctx_pos == source, cached_rows(row), block)
        pairs = [(source, dest) for source, (_, dest, _) in step.items()]
        sent.append(block)
        later.append(lax.ppermute(block, "ctx", pairs))
        picks.append([(dest, slot) for _, dest, slot in step.values()])

    near, *_ = lax.optimization_barrier((near, *sent[::-1]))
    if kv_cols != all_cols:
        at = (1 - sub_pos) * kv_cols
        near_theirs = jnp.concatenate(
            [
                lax.dynamic_slice_in_dim(near, at, kv_cols, 1),
                lax.dynamic_slice_in_dim(near, at + all_cols, kv_cols, 1),
            ],
            axis=1,
        )
    else:
        near_theirs = near
    far = swap_cores(near_theirs)
    mine_q = lax.dynamic_slice_in_dim(queries, sub_pos * head_cols, head_cols, 1)
    return pl.pallas_call(
        functools.partial(window_kernel, picks),
        out_shape=jax.ShapeDtypeStruct((tok_rows, head_cols), queries.dtype),
        in_specs=[vmem] * (6 + len(later)),
        out_specs=vmem,
        compiler_params=pltpu.CompilerParams(vmem_limit_bytes=24 << 20),
    )(mine_q, bias, mine, peers, near, far, *later)


def solution(mesh):
    in_specs = (
        P(("grp", "ctx"), "head"),
        P(("grp", "ctx", "sub"), "head"),
        P(("grp", "ctx", "sub"), "head"),
        P(("grp", "ctx", "sub"), "head"),
        P(("grp", "ctx", "sub"), "head"),
        P("grp"),
    )
    out_specs = P(("grp", "ctx"), ("head", "sub"))
    return jax.shard_map(
        on_device, mesh=mesh, in_specs=in_specs, out_specs=out_specs, check_vma=False
    )
```

```python
import functools
import math

import jax
import jax.numpy as jnp
from jax import lax
from jax.experimental import pallas as pl
from jax.experimental.pallas import tpu as pltpu
from jax.sharding import PartitionSpec as P

HEAD_DIM = 128
NEG_FILL = -1e30
SCORE_SCALE = HEAD_DIM ** (-0.5)
EXP2_SCALE = SCORE_SCALE * math.log2(math.e)
HEADS_AT_ONCE = 8


def swap_cores(x):
    return lax.ppermute(x, "sub", [(0, 1), (1, 0)])


def pack_kernel(n_ctx, first_sender, k_ref, v_ref, ck_ref, cv_ref, raw_ref, mine_ref, theirs_ref, sems):
    sub_pos = lax.axis_index("sub")
    last = lax.axis_index("ctx") == n_ctx - 1
    stretch_part, all_cols = k_ref.shape
    cache_part = ck_ref.shape[0]
    kv_cols = mine_ref.shape[1] // 2
    split = kv_cols != all_cols
    sends_cached = lax.axis_index("ctx") >= first_sender
    copies, cached = [], []
    for i, (own_src, cache_src) in enumerate([(k_ref, ck_ref), (v_ref, cv_ref)]):
        dst = raw_ref.at[:, pl.ds(i * all_cols, all_cols)]
        from_own = pltpu.make_async_copy(own_src, dst, sems.at[0, i])
        tail = cache_src.at[pl.ds(cache_part - stretch_part, stretch_part), :]
        from_cache = pltpu.make_async_copy(tail, dst, sems.at[0, i])
        pl.when(last)(from_cache.start)
        pl.when(jnp.logical_not(last))(from_own.start)
        copies.append(from_own)
    for out, owner in ((2, 1 - sub_pos), (1, sub_pos)):
        dst = (None, mine_ref, theirs_ref)[out]
        at = pl.multiple_of(owner * kv_cols, HEAD_DIM) if split else 0
        for i, (src, row, rows, col) in enumerate([
            (k_ref, 0, stretch_part, 0),
            (v_ref, 0, stretch_part, kv_cols),
            (ck_ref, stretch_part, cache_part, 0),
            (cv_ref, stretch_part, cache_part, kv_cols),
        ]):
            copy = pltpu.make_async_copy(
                src.at[:, pl.ds(at, kv_cols)],
                dst.at[pl.ds(row, rows), pl.ds(col, kv_cols)],
                sems.at[out, i],
            )
            if i < 2:
                copy.start()
                copies.append(copy)
            else:
                pl.when(sends_cached)(copy.start)
                cached.append(copy)
    for copy in copies:
        copy.wait()
    for copy in cached:
        pl.when(sends_cached)(copy.wait)


def bias_kernel(prefix_len, stretch_part, cache_part, len_ref, bias_ref, lengths, sem):
    copy = pltpu.make_async_copy(len_ref, lengths, sem)
    copy.start()
    sub_pos, ctx_pos = lax.axis_index("sub"), lax.axis_index("ctx")
    tok_rows = bias_ref.shape[0]
    n_sub = tok_rows // stretch_part
    first = prefix_len + ctx_pos * tok_rows
    row = lax.broadcasted_iota(jnp.int32, (tok_rows, tok_rows), 0)
    lane = lax.broadcasted_iota(jnp.int32, (tok_rows, tok_rows), 1)
    doc_start = jnp.zeros((tok_rows, tok_rows), jnp.int32)
    copy.wait()
    end = jnp.int32(0)
    for doc in range(lengths.shape[0]):
        end = end + lengths[doc]
        doc_start = jnp.where(first + row >= end, end, doc_start)
    for slot in range(bias_ref.shape[1] // tok_rows):
        at = first - slot * tok_rows
        low, high = at + sub_pos * stretch_part, at + (1 - sub_pos) * stretch_part
        if slot == 1:
            tail = prefix_len - (n_sub - 1) * cache_part - stretch_part
            low = jnp.where(ctx_pos == 0, tail + sub_pos * cache_part, low)
            high = jnp.where(ctx_pos == 0, tail + (1 - sub_pos) * cache_part, high)
        elif slot > 1:
            at = jnp.where(ctx_pos == 0, prefix_len - cache_part, at) if slot == 2 else at
            low = jnp.where(ctx_pos < slot, at, low)
            high = jnp.where(ctx_pos < slot, at + stretch_part, high)
        key = jnp.where(lane < stretch_part, low + lane, high + lane - stretch_part)
        allowed = key >= doc_start
        if slot == 0:
            allowed = allowed & (key <= first + row)
        bias_ref[:, slot * tok_rows : (slot + 1) * tok_rows] = jnp.where(allowed, 0.0, NEG_FILL)


def stacked(ref, heads):
    return jnp.concatenate([ref[:, h * HEAD_DIM : (h + 1) * HEAD_DIM] for h in heads], axis=0)


def attend(q_ref, bias, block, group, heads):
    kv_cols = block.shape[1] // 2
    at = group * HEAD_DIM
    keys, values = block[:, at : at + HEAD_DIM], block[:, kv_cols + at : kv_cols + at + HEAD_DIM]
    scores = lax.dot_general(
        stacked(q_ref, heads), keys, (((1,), (1,)), ((), ())), preferred_element_type=jnp.float32
    )
    scores = scores.reshape(len(heads), *bias.shape) + bias[None]
    ones = jnp.ones_like(values)
    return scores.reshape(-1, bias.shape[1]), jnp.concatenate([values, ones], axis=1)


def weigh(scores, row_max, values):
    rounded = jnp.exp2((scores - row_max) * EXP2_SCALE).astype(jnp.bfloat16)
    summed = jnp.dot(rounded, values, preferred_element_type=jnp.float32)
    return summed[:, :HEAD_DIM], summed[:, HEAD_DIM:]


def near_kernel(q_ref, bias_ref, own_ref, peer_ref, near_ref, far_ref, max_ref, sum_ref, out_ref):
    stretch_part, kv_cols = near_ref.shape[0], own_ref.shape[1] // 2
    all_cols = near_ref.shape[1] // 2
    at = [0, all_cols]
    if all_cols != kv_cols:
        at = [pl.multiple_of(lax.axis_index("sub") * kv_cols + x, HEAD_DIM) for x in at]
    near = jnp.concatenate([near_ref[:, pl.ds(x, kv_cols)] for x in at], axis=1)
    block = jnp.concatenate(
        [own_ref[:stretch_part], peer_ref[:stretch_part], near, far_ref[...]], axis=0
    )
    tok_rows, head_cols = q_ref.shape
    per_group = head_cols // kv_cols
    bias = bias_ref[:, : block.shape[0]]
    for first in range(0, head_cols // HEAD_DIM, HEADS_AT_ONCE):
        heads = range(first, min(first + HEADS_AT_ONCE, head_cols // HEAD_DIM))
        scores, values = attend(q_ref, bias, block, first // per_group, heads)
        row_max = jnp.max(scores, axis=1, keepdims=True)
        weighted, row_sum = weigh(scores, row_max, values)
        row_max = jnp.broadcast_to(row_max, weighted.shape)
        for i, head in enumerate(heads):
            here, rows = pl.ds(head * HEAD_DIM, HEAD_DIM), slice(i * tok_rows, (i + 1) * tok_rows)
            max_ref[:, here] = row_max[rows]
            sum_ref[:, here] = row_sum[rows]
            out_ref[:, here] = weighted[rows]


def later_kernel(picks, q_ref, bias_ref, max_ref, sum_ref, weighted_ref, *refs):
    later_refs, (o_ref, out, sems) = refs[:-3], refs[-3:]
    ctx_pos = lax.axis_index("ctx")
    tok_rows, head_cols = q_ref.shape
    blocks = [None] * (bias_ref.shape[1] // tok_rows)
    for later_ref, pick in zip(later_refs, picks):
        for slot in sorted({slot for _, slot in pick}):
            here = [ctx_pos == dest for dest, at in pick if at == slot]
            block = later_ref[...]
            if blocks[slot] is not None:
                block = jnp.where(functools.reduce(jnp.logical_or, here), block, blocks[slot])
            blocks[slot] = block
    block = jnp.concatenate(blocks[2:], axis=0)
    per_group = head_cols // (block.shape[1] // 2)
    bias = bias_ref[:, 2 * tok_rows :]
    copies = []
    for first in range(0, head_cols // HEAD_DIM, HEADS_AT_ONCE):
        heads = range(first, min(first + HEADS_AT_ONCE, head_cols // HEAD_DIM))
        scores, values = attend(q_ref, bias, block, first // per_group, heads)
        old_max = stacked(max_ref, heads)
        row_max = jnp.maximum(old_max, jnp.max(scores, axis=1, keepdims=True))
        wide_max = jnp.concatenate([row_max] * (block.shape[0] // HEAD_DIM), axis=1)
        weighted, row_sum = weigh(scores, wide_max, values)
        shrink = jnp.exp2((old_max - row_max) * EXP2_SCALE)
        weighted = stacked(weighted_ref, heads) * shrink + weighted
        row_sum = stacked(sum_ref, heads) * shrink + row_sum
        result = (weighted * pl.reciprocal(row_sum, approx=True)).astype(out.dtype)
        for i, head in enumerate(heads):
            here = pl.ds(head * HEAD_DIM, HEAD_DIM)
            out[:, here] = result[i * tok_rows : (i + 1) * tok_rows]
        here = pl.ds(first * HEAD_DIM, len(heads) * HEAD_DIM)
        copy = pltpu.make_async_copy(out.at[:, here], o_ref.at[:, here], sems.at[len(copies)])
        copy.start()
        copies.append(copy)
    for copy in copies:
        copy.wait()


def plan_rounds(n_ctx, reach, tok_rows, cache_part, shard_rows):
    per_shard = shard_rows // tok_rows
    cached, stretch = [], []
    for dest in range(n_ctx):
        for slot in range(2, reach + 1):
            back = slot - dest
            if back <= 0:
                stretch.append((dest - slot, None, dest, slot))
                continue
            source = n_ctx - 1 - (back - 1) // per_shard
            row = shard_rows - ((back - 1) % per_shard + 1) * tok_rows
            if dest == 0 and back == 2:
                row = cache_part
            cached.append((source, row, dest, slot))
    rounds = []
    for source, row, dest, slot in cached + stretch:
        dests = [{d for _, d, _ in step.values()} for step in rounds]
        free = [i for i, step in enumerate(rounds) if source not in step and dest not in dests[i]]
        free.sort(key=lambda i: source not in dests[i])
        if not free:
            rounds.append({})
            free = [len(rounds) - 1]
        rounds[free[0]][source] = (row, dest, slot)
    return rounds


def on_device(queries, stretch_keys, stretch_values, cache_keys, cache_values, doc_lengths):
    n_ctx = lax.axis_size("ctx")
    n_sub = lax.axis_size("sub")
    ctx_pos = lax.axis_index("ctx")
    sub_pos = lax.axis_index("sub")
    tok_rows = queries.shape[0]
    stretch_part, all_cols = stretch_keys.shape
    cache_part = cache_keys.shape[0]
    prefix_len = cache_part * n_sub * n_ctx
    head_cols = queries.shape[1] // n_sub
    reach = n_ctx // 2
    assert cache_part == 3 * stretch_part and tok_rows == 2 * stretch_part
    kv_cols = all_cols // n_sub if all_cols // HEAD_DIM % n_sub == 0 else all_cols
    vmem = pl.BlockSpec(memory_space=pltpu.VMEM)
    hbm = pl.BlockSpec(memory_space=pltpu.HBM)
    small = pltpu.CompilerParams(vmem_limit_bytes=8 << 20)

    def in_hbm(*arrays):
        return [pltpu.with_memory_space_constraint(x, pltpu.HBM) for x in arrays]

    rounds = plan_rounds(n_ctx, reach, tok_rows, cache_part, cache_part * n_sub)
    first_sender = min(src for step in rounds for src, sent in step.items() if sent[0] is not None)
    half = jax.ShapeDtypeStruct((stretch_part + cache_part, 2 * kv_cols), stretch_keys.dtype)
    raw, mine, theirs = pl.pallas_call(
        functools.partial(pack_kernel, n_ctx, first_sender),
        out_shape=[
            jax.ShapeDtypeStruct((stretch_part, 2 * all_cols), stretch_keys.dtype), half, half
        ],
        in_specs=[hbm] * 4,
        out_specs=[vmem] * 3,
        scratch_shapes=[pltpu.SemaphoreType.DMA((3, 4))],
        compiler_params=small,
    )(*in_hbm(stretch_keys, stretch_values, cache_keys, cache_values))
    bias = pl.pallas_call(
        functools.partial(bias_kernel, prefix_len, stretch_part, cache_part),
        out_shape=jax.ShapeDtypeStruct((tok_rows, (reach + 1) * tok_rows), jnp.float32),
        in_specs=[hbm],
        out_specs=vmem,
        scratch_shapes=[pltpu.SMEM(doc_lengths.shape, jnp.int32), pltpu.SemaphoreType.DMA],
        compiler_params=small,
    )(*in_hbm(doc_lengths))

    peers = swap_cores(theirs)
    near = lax.ppermute(raw, "ctx", [(i, (i + 1) % n_ctx) for i in range(n_ctx)])

    def cached_rows(row):
        parts = []
        for owner in range(n_sub):
            low = max(row, owner * cache_part) - owner * cache_part + stretch_part
            high = min(row + tok_rows, (owner + 1) * cache_part) - owner * cache_part + stretch_part
            if low < high:
                parts.append(jnp.where(sub_pos == owner, mine[low:high], peers[low:high]))
        return jnp.concatenate(parts) if len(parts) > 1 else parts[0]

    own = jnp.concatenate([mine[:stretch_part], peers[:stretch_part]])
    sent, later, picks = [], [], []
    for step in rounds:
        block = own
        for source, (row, _, _) in step.items():
            if row is not None:
                block = jnp.where(ctx_pos == source, cached_rows(row), block)
        pairs = [(source, dest) for source, (_, dest, _) in step.items()]
        sent.append(block)
        later.append(lax.ppermute(block, "ctx", pairs))
        picks.append([(dest, slot) for _, dest, slot in step.values()])

    near, *_ = lax.optimization_barrier((near, *sent[::-1]))
    if kv_cols != all_cols:
        at = (1 - sub_pos) * kv_cols
        near_theirs = jnp.concatenate(
            [
                lax.dynamic_slice_in_dim(near, at, kv_cols, 1),
                lax.dynamic_slice_in_dim(near, at + all_cols, kv_cols, 1),
            ],
            axis=1,
        )
    else:
        near_theirs = near
    far = swap_cores(near_theirs)
    mine_q = lax.dynamic_slice_in_dim(queries, sub_pos * head_cols, head_cols, 1)
    head_count = head_cols // HEAD_DIM
    state = jax.ShapeDtypeStruct((tok_rows, head_cols), jnp.float32)
    large = pltpu.CompilerParams(vmem_limit_bytes=24 << 20)
    row_max, row_sum, weighted = pl.pallas_call(
        near_kernel,
        out_shape=[state] * 3,
        in_specs=[vmem] * 6,
        out_specs=[vmem] * 3,
        compiler_params=large,
    )(mine_q, bias, mine, peers, near, far)
    return pl.pallas_call(
        functools.partial(later_kernel, picks),
        out_shape=jax.ShapeDtypeStruct((tok_rows, head_cols), queries.dtype),
        in_specs=[vmem] * (5 + len(later)),
        out_specs=hbm,
        scratch_shapes=[
            pltpu.VMEM((tok_rows, head_cols), queries.dtype),
            pltpu.SemaphoreType.DMA((pl.cdiv(head_count, HEADS_AT_ONCE),)),
        ],
        compiler_params=large,
    )(mine_q, bias, row_max, row_sum, weighted, *later)


def solution(mesh):
    in_specs = (
        P(("grp", "ctx"), "head"),
        P(("grp", "ctx", "sub"), "head"),
        P(("grp", "ctx", "sub"), "head"),
        P(("grp", "ctx", "sub"), "head"),
        P(("grp", "ctx", "sub"), "head"),
        P("grp"),
    )
    out_specs = P(("grp", "ctx"), ("head", "sub"))
    return jax.shard_map(
        on_device, mesh=mesh, in_specs=in_specs, out_specs=out_specs, check_vma=False
    )
```

```python
import functools
import math

import jax
import jax.numpy as jnp
from jax import lax
from jax.experimental import pallas as pl
from jax.experimental.pallas import tpu as pltpu
from jax.sharding import PartitionSpec as P

HEAD_DIM = 128
NEG_FILL = -1e30
SCORE_SCALE = HEAD_DIM ** (-0.5)
EXP2_SCALE = SCORE_SCALE * math.log2(math.e)
HEADS_AT_ONCE = 8
LATER_HEADS = 2


def swap_cores(x):
    return lax.ppermute(x, "sub", [(0, 1), (1, 0)])


def pack_kernel(n_ctx, first_sender, k_ref, v_ref, ck_ref, cv_ref, raw_ref, mine_ref, theirs_ref, sems):
    sub_pos = lax.axis_index("sub")
    last = lax.axis_index("ctx") == n_ctx - 1
    stretch_part, all_cols = k_ref.shape
    cache_part = ck_ref.shape[0]
    kv_cols = mine_ref.shape[1] // 2
    split = kv_cols != all_cols
    sends_cached = lax.axis_index("ctx") >= first_sender
    copies, cached = [], []
    for i, (own_src, cache_src) in enumerate([(k_ref, ck_ref), (v_ref, cv_ref)]):
        dst = raw_ref.at[:, pl.ds(i * all_cols, all_cols)]
        from_own = pltpu.make_async_copy(own_src, dst, sems.at[0, i])
        tail = cache_src.at[pl.ds(cache_part - stretch_part, stretch_part), :]
        from_cache = pltpu.make_async_copy(tail, dst, sems.at[0, i])
        pl.when(last)(from_cache.start)
        pl.when(jnp.logical_not(last))(from_own.start)
        copies.append(from_own)
    for out, owner in ((2, 1 - sub_pos), (1, sub_pos)):
        dst = (None, mine_ref, theirs_ref)[out]
        at = pl.multiple_of(owner * kv_cols, HEAD_DIM) if split else 0
        for i, (src, row, rows, col) in enumerate([
            (k_ref, 0, stretch_part, 0),
            (v_ref, 0, stretch_part, kv_cols),
            (ck_ref, stretch_part, cache_part, 0),
            (cv_ref, stretch_part, cache_part, kv_cols),
        ]):
            copy = pltpu.make_async_copy(
                src.at[:, pl.ds(at, kv_cols)],
                dst.at[pl.ds(row, rows), pl.ds(col, kv_cols)],
                sems.at[out, i],
            )
            if i < 2:
                copy.start()
                copies.append(copy)
            else:
                pl.when(sends_cached)(copy.start)
                cached.append(copy)
    for copy in copies:
        copy.wait()
    for copy in cached:
        pl.when(sends_cached)(copy.wait)


def bias_kernel(prefix_len, stretch_part, cache_part, len_ref, bias_ref, lengths, sem):
    copy = pltpu.make_async_copy(len_ref, lengths, sem)
    copy.start()
    sub_pos, ctx_pos = lax.axis_index("sub"), lax.axis_index("ctx")
    tok_rows = bias_ref.shape[0]
    n_sub = tok_rows // stretch_part
    first = prefix_len + ctx_pos * tok_rows
    row = lax.broadcasted_iota(jnp.int32, (tok_rows, tok_rows), 0)
    lane = lax.broadcasted_iota(jnp.int32, (tok_rows, tok_rows), 1)
    doc_start = jnp.zeros((tok_rows, tok_rows), jnp.int32)
    copy.wait()
    end = jnp.int32(0)
    for doc in range(lengths.shape[0]):
        end = end + lengths[doc]
        doc_start = jnp.where(first + row >= end, end, doc_start)
    for slot in range(bias_ref.shape[1] // tok_rows):
        at = first - slot * tok_rows
        low, high = at + sub_pos * stretch_part, at + (1 - sub_pos) * stretch_part
        if slot == 1:
            tail = prefix_len - (n_sub - 1) * cache_part - stretch_part
            low = jnp.where(ctx_pos == 0, tail + sub_pos * cache_part, low)
            high = jnp.where(ctx_pos == 0, tail + (1 - sub_pos) * cache_part, high)
        elif slot > 1:
            at = jnp.where(ctx_pos == 0, prefix_len - cache_part, at) if slot == 2 else at
            low = jnp.where(ctx_pos < slot, at, low)
            high = jnp.where(ctx_pos < slot, at + stretch_part, high)
        key = jnp.where(lane < stretch_part, low + lane, high + lane - stretch_part)
        allowed = key >= doc_start
        if slot == 0:
            allowed = allowed & (key <= first + row)
        bias_ref[:, slot * tok_rows : (slot + 1) * tok_rows] = jnp.where(allowed, 0.0, NEG_FILL)


def stacked(ref, heads):
    return jnp.concatenate([ref[:, h * HEAD_DIM : (h + 1) * HEAD_DIM] for h in heads], axis=0)


def attend(q_ref, bias, block, group, heads):
    kv_cols = block.shape[1] // 2
    at = group * HEAD_DIM
    keys, values = block[:, at : at + HEAD_DIM], block[:, kv_cols + at : kv_cols + at + HEAD_DIM]
    scores = lax.dot_general(
        stacked(q_ref, heads), keys, (((1,), (1,)), ((), ())), preferred_element_type=jnp.float32
    )
    scores = scores.reshape(len(heads), *bias.shape) + bias[None]
    ones = jnp.ones_like(values)
    return scores.reshape(-1, bias.shape[1]), jnp.concatenate([values, ones], axis=1)


def weigh(scores, row_max, values):
    rounded = jnp.exp2((scores - row_max) * EXP2_SCALE).astype(jnp.bfloat16)
    summed = jnp.dot(rounded, values, preferred_element_type=jnp.float32)
    return summed[:, :HEAD_DIM], summed[:, HEAD_DIM:]


def near_kernel(q_ref, bias_ref, own_ref, peer_ref, near_ref, far_ref, max_ref, sum_ref, out_ref):
    stretch_part, kv_cols = near_ref.shape[0], own_ref.shape[1] // 2
    all_cols = near_ref.shape[1] // 2
    at = [0, all_cols]
    if all_cols != kv_cols:
        at = [pl.multiple_of(lax.axis_index("sub") * kv_cols + x, HEAD_DIM) for x in at]
    near = jnp.concatenate([near_ref[:, pl.ds(x, kv_cols)] for x in at], axis=1)
    block = jnp.concatenate(
        [own_ref[:stretch_part], peer_ref[:stretch_part], near, far_ref[...]], axis=0
    )
    tok_rows, head_cols = q_ref.shape
    per_group = head_cols // kv_cols
    bias = bias_ref[:, : block.shape[0]]
    for first in range(0, head_cols // HEAD_DIM, HEADS_AT_ONCE):
        heads = range(first, min(first + HEADS_AT_ONCE, head_cols // HEAD_DIM))
        scores, values = attend(q_ref, bias, block, first // per_group, heads)
        row_max = jnp.max(scores, axis=1, keepdims=True)
        weighted, row_sum = weigh(scores, row_max, values)
        row_max = jnp.broadcast_to(row_max, weighted.shape)
        for i, head in enumerate(heads):
            here, rows = pl.ds(head * HEAD_DIM, HEAD_DIM), slice(i * tok_rows, (i + 1) * tok_rows)
            max_ref[:, here] = row_max[rows]
            sum_ref[:, here] = row_sum[rows]
            out_ref[:, here] = weighted[rows]


def later_kernel(picks, q_ref, bias_ref, max_ref, sum_ref, weighted_ref, *refs):
    later_refs, (o_ref, out, sems) = refs[:-3], refs[-3:]
    ctx_pos, sub_pos = lax.axis_index("ctx"), lax.axis_index("sub")
    tok_rows, head_cols = q_ref.shape
    blocks = [None] * (bias_ref.shape[1] // tok_rows)
    for later_ref, pick in zip(later_refs, picks):
        for slot in sorted({slot for _, _, slot in pick}):
            here = [(ctx_pos == dest) & (sub_pos == sub) for dest, sub, at in pick if at == slot]
            block = later_ref[...]
            if blocks[slot] is not None:
                block = jnp.where(functools.reduce(jnp.logical_or, here), block, blocks[slot])
            blocks[slot] = block
    block = jnp.concatenate(blocks[2:], axis=0)
    per_group = head_cols // (block.shape[1] // 2)
    bias = bias_ref[:, 2 * tok_rows :]
    head_count = head_cols // HEAD_DIM
    batches = [
        range(first, min(first + LATER_HEADS, head_count))
        for first in range(0, head_count, LATER_HEADS)
    ]
    attended = [attend(q_ref, bias, block, heads[0] // per_group, heads) for heads in batches]
    copies = []
    for heads, (scores, values) in zip(batches, attended):
        old_max = stacked(max_ref, heads)
        row_max = jnp.maximum(old_max, jnp.max(scores, axis=1, keepdims=True))
        wide_max = jnp.concatenate([row_max] * (block.shape[0] // HEAD_DIM), axis=1)
        weighted, row_sum = weigh(scores, wide_max, values)
        shrink = jnp.exp2((old_max - row_max) * EXP2_SCALE)
        weighted = stacked(weighted_ref, heads) * shrink + weighted
        row_sum = stacked(sum_ref, heads) * shrink + row_sum
        result = (weighted * pl.reciprocal(row_sum, approx=True)).astype(out.dtype)
        for i, head in enumerate(heads):
            here = pl.ds(head * HEAD_DIM, HEAD_DIM)
            out[:, here] = result[i * tok_rows : (i + 1) * tok_rows]
        here = pl.ds(heads[0] * HEAD_DIM, len(heads) * HEAD_DIM)
        copy = pltpu.make_async_copy(out.at[:, here], o_ref.at[:, here], sems.at[len(copies)])
        copy.start()
        copies.append(copy)
    for copy in copies:
        copy.wait()


def plan_rounds(n_ctx, n_sub, reach, tok_rows, cache_part, shard_rows):
    per_shard = shard_rows // tok_rows
    cached, stretch = [], []
    for dest in range(n_ctx):
        for slot in range(2, reach + 1):
            back = slot - dest
            if back <= 0:
                stretch.append((dest - slot, None, dest, slot))
                continue
            source = n_ctx - 1 - (back - 1) // per_shard
            row = shard_rows - ((back - 1) % per_shard + 1) * tok_rows
            if dest == 0 and back == 2:
                row = cache_part
            cached.append((source, row, dest, slot))
    rounds = []
    for source, row, dest, slot in cached + stretch:
        for sub in range(n_sub):
            dests = [{(d, i) for (_, i), (_, d, _) in step.items()} for step in rounds]
            free = [
                i for i, step in enumerate(rounds)
                if (source, sub) not in step and (dest, sub) not in dests[i]
            ]
            free.sort(key=lambda i: ((source, sub) in dests[i]) == (sub > 0))
            if not free:
                rounds.append({})
                free = [len(rounds) - 1]
            rounds[free[0]][source, sub] = (row, dest, slot)
    return rounds


def on_device(queries, stretch_keys, stretch_values, cache_keys, cache_values, doc_lengths):
    n_ctx = lax.axis_size("ctx")
    n_sub = lax.axis_size("sub")
    ctx_pos = lax.axis_index("ctx")
    sub_pos = lax.axis_index("sub")
    tok_rows = queries.shape[0]
    stretch_part, all_cols = stretch_keys.shape
    cache_part = cache_keys.shape[0]
    prefix_len = cache_part * n_sub * n_ctx
    head_cols = queries.shape[1] // n_sub
    reach = n_ctx // 2
    assert cache_part == 3 * stretch_part and tok_rows == 2 * stretch_part
    kv_cols = all_cols // n_sub if all_cols // HEAD_DIM % n_sub == 0 else all_cols
    vmem = pl.BlockSpec(memory_space=pltpu.VMEM)
    hbm = pl.BlockSpec(memory_space=pltpu.HBM)
    small = pltpu.CompilerParams(vmem_limit_bytes=8 << 20)

    def in_hbm(*arrays):
        return [pltpu.with_memory_space_constraint(x, pltpu.HBM) for x in arrays]

    rounds = plan_rounds(n_ctx, n_sub, reach, tok_rows, cache_part, cache_part * n_sub)
    first_sender = min(src for step in rounds for (src, _), leg in step.items() if leg[0] is not None)
    half = jax.ShapeDtypeStruct((stretch_part + cache_part, 2 * kv_cols), stretch_keys.dtype)
    raw, mine, theirs = pl.pallas_call(
        functools.partial(pack_kernel, n_ctx, first_sender),
        out_shape=[
            jax.ShapeDtypeStruct((stretch_part, 2 * all_cols), stretch_keys.dtype), half, half
        ],
        in_specs=[hbm] * 4,
        out_specs=[vmem] * 3,
        scratch_shapes=[pltpu.SemaphoreType.DMA((3, 4))],
        compiler_params=small,
    )(*in_hbm(stretch_keys, stretch_values, cache_keys, cache_values))
    bias = pl.pallas_call(
        functools.partial(bias_kernel, prefix_len, stretch_part, cache_part),
        out_shape=jax.ShapeDtypeStruct((tok_rows, (reach + 1) * tok_rows), jnp.float32),
        in_specs=[hbm],
        out_specs=vmem,
        scratch_shapes=[pltpu.SMEM(doc_lengths.shape, jnp.int32), pltpu.SemaphoreType.DMA],
        compiler_params=small,
    )(*in_hbm(doc_lengths))

    peers = swap_cores(theirs)
    near = lax.ppermute(raw, "ctx", [(i, (i + 1) % n_ctx) for i in range(n_ctx)])

    def cached_rows(row):
        parts = []
        for owner in range(n_sub):
            low = max(row, owner * cache_part) - owner * cache_part + stretch_part
            high = min(row + tok_rows, (owner + 1) * cache_part) - owner * cache_part + stretch_part
            if low < high:
                parts.append(jnp.where(sub_pos == owner, mine[low:high], peers[low:high]))
        return jnp.concatenate(parts) if len(parts) > 1 else parts[0]

    own = jnp.concatenate([mine[:stretch_part], peers[:stretch_part]])
    sent, later, picks = [], [], []
    for step in rounds:
        block = own
        for source, row in sorted({(src, leg[0]) for (src, _), leg in step.items() if leg[0] is not None}):
            block = jnp.where(ctx_pos == source, cached_rows(row), block)
        pairs = [(src * n_sub + sub, leg[1] * n_sub + sub) for (src, sub), leg in step.items()]
        sent.append(block)
        later.append(lax.ppermute(block, ("ctx", "sub"), pairs))
        picks.append([(dest, sub, slot) for (_, sub), (_, dest, slot) in step.items()])

    near, *_ = lax.optimization_barrier((near, *sent[::-1]))
    if kv_cols != all_cols:
        at = (1 - sub_pos) * kv_cols
        near_theirs = jnp.concatenate(
            [
                lax.dynamic_slice_in_dim(near, at, kv_cols, 1),
                lax.dynamic_slice_in_dim(near, at + all_cols, kv_cols, 1),
            ],
            axis=1,
        )
    else:
        near_theirs = near
    far = swap_cores(near_theirs)
    mine_q = lax.dynamic_slice_in_dim(queries, sub_pos * head_cols, head_cols, 1)
    head_count = head_cols // HEAD_DIM
    state = jax.ShapeDtypeStruct((tok_rows, head_cols), jnp.float32)
    large = pltpu.CompilerParams(vmem_limit_bytes=24 << 20)
    row_max, row_sum, weighted = pl.pallas_call(
        near_kernel,
        out_shape=[state] * 3,
        in_specs=[vmem] * 6,
        out_specs=[vmem] * 3,
        compiler_params=large,
    )(mine_q, bias, mine, peers, near, far)
    return pl.pallas_call(
        functools.partial(later_kernel, picks),
        out_shape=jax.ShapeDtypeStruct((tok_rows, head_cols), queries.dtype),
        in_specs=[vmem] * (5 + len(later)),
        out_specs=hbm,
        scratch_shapes=[
            pltpu.VMEM((tok_rows, head_cols), queries.dtype),
            pltpu.SemaphoreType.DMA((pl.cdiv(head_count, LATER_HEADS),)),
        ],
        compiler_params=large,
    )(mine_q, bias, row_max, row_sum, weighted, *later)


def solution(mesh):
    in_specs = (
        P(("grp", "ctx"), "head"),
        P(("grp", "ctx", "sub"), "head"),
        P(("grp", "ctx", "sub"), "head"),
        P(("grp", "ctx", "sub"), "head"),
        P(("grp", "ctx", "sub"), "head"),
        P("grp"),
    )
    out_specs = P(("grp", "ctx"), ("head", "sub"))
    return jax.shard_map(
        on_device, mesh=mesh, in_specs=in_specs, out_specs=out_specs, check_vma=False
    )
```

```python
import functools
import math

import jax
import jax.numpy as jnp
from jax import lax
from jax.experimental import pallas as pl
from jax.experimental.pallas import tpu as pltpu
from jax.sharding import PartitionSpec as P

HEAD_DIM = 128
NEG_FILL = -1e30
SCORE_SCALE = HEAD_DIM ** (-0.5)
EXP2_SCALE = SCORE_SCALE * math.log2(math.e)
HEADS_AT_ONCE = 8
LATER_HEADS = 2


def swap_cores(x):
    return lax.ppermute(x, "sub", [(0, 1), (1, 0)])


def pack_kernel(n_ctx, owners, k_ref, v_ref, ck_ref, cv_ref, raw_ref, mine_ref, theirs_ref, sems):
    ctx_pos, sub_pos = lax.axis_index("ctx"), lax.axis_index("sub")
    last = ctx_pos == n_ctx - 1
    owns = functools.reduce(jnp.logical_or, [(ctx_pos == c) & (sub_pos == s) for c, s in owners])
    stretch_part, all_cols = k_ref.shape
    cache_part = ck_ref.shape[0]
    kv_cols = mine_ref.shape[1] // 2
    for i, (own_src, cache_src) in enumerate([(k_ref, ck_ref), (v_ref, cv_ref)]):
        dst = raw_ref.at[:, pl.ds(i * all_cols, all_cols)]
        from_own = pltpu.make_async_copy(own_src, dst, sems.at[0])
        tail = cache_src.at[pl.ds(cache_part - stretch_part, stretch_part), :]
        from_cache = pltpu.make_async_copy(tail, dst, sems.at[0])
        pl.when(last)(from_cache.start)
        pl.when(jnp.logical_not(last))(from_own.start)
    cached = pl.ds(stretch_part, cache_part)
    for n, (dst, owner) in enumerate([(theirs_ref, 1 - sub_pos), (mine_ref, sub_pos)]):
        at = pl.multiple_of(owner * kv_cols, HEAD_DIM) if kv_cols != all_cols else 0
        for src, rows, col, sem in [
            (k_ref, pl.ds(0, stretch_part), 0, 0),
            (v_ref, pl.ds(0, stretch_part), kv_cols, 0),
            (ck_ref, cached, 0, 1 + n),
            (cv_ref, cached, kv_cols, 1 + n),
        ]:
            part = src.at[:, pl.ds(at, kv_cols)]
            copy = pltpu.make_async_copy(part, dst.at[rows, pl.ds(col, kv_cols)], sems.at[sem])
            if sem:
                pl.when(owns)(copy.start)
            else:
                copy.start()

    def wait_for(rows, sem):
        pltpu.make_async_copy(mine_ref.at[rows, :], mine_ref.at[rows, :], sems.at[sem]).wait()

    @pl.when(owns)
    def _():
        wait_for(cached, 1)
        wait_for(cached, 2)

    wait_for(pl.ds(0, stretch_part * (all_cols + 2 * kv_cols) // kv_cols), 0)


def bias_kernel(prefix_len, stretch_part, cache_part, len_ref, bias_ref, lengths, sem):
    copy = pltpu.make_async_copy(len_ref, lengths, sem)
    copy.start()
    sub_pos, ctx_pos = lax.axis_index("sub"), lax.axis_index("ctx")
    tok_rows = bias_ref.shape[0]
    n_sub = tok_rows // stretch_part
    first = prefix_len + ctx_pos * tok_rows
    row = lax.broadcasted_iota(jnp.int32, (tok_rows, tok_rows), 0)
    lane = lax.broadcasted_iota(jnp.int32, (tok_rows, tok_rows), 1)
    doc_start = jnp.zeros((tok_rows, tok_rows), jnp.int32)
    copy.wait()
    end = jnp.int32(0)
    for doc in range(lengths.shape[0]):
        end = end + lengths[doc]
        doc_start = jnp.where(first + row >= end, end, doc_start)
    for slot in range(bias_ref.shape[1] // tok_rows):
        at = first - slot * tok_rows
        low, high = at + sub_pos * stretch_part, at + (1 - sub_pos) * stretch_part
        if slot == 1:
            tail = prefix_len - (n_sub - 1) * cache_part - stretch_part
            low = jnp.where(ctx_pos == 0, tail + sub_pos * cache_part, low)
            high = jnp.where(ctx_pos == 0, tail + (1 - sub_pos) * cache_part, high)
        elif slot > 1:
            at = jnp.where(ctx_pos == 0, prefix_len - cache_part, at) if slot == 2 else at
            low = jnp.where(ctx_pos < slot, at, low)
            high = jnp.where(ctx_pos < slot, at + stretch_part, high)
        key = jnp.where(lane < stretch_part, low + lane, high + lane - stretch_part)
        allowed = key >= doc_start
        if slot == 0:
            allowed = allowed & (key <= first + row)
        bias_ref[:, slot * tok_rows : (slot + 1) * tok_rows] = jnp.where(allowed, 0.0, NEG_FILL)


def stacked(ref, heads):
    return jnp.concatenate([ref[:, h * HEAD_DIM : (h + 1) * HEAD_DIM] for h in heads], axis=0)


def attend(q_ref, bias, block, group, heads):
    kv_cols = block.shape[1] // 2
    at = group * HEAD_DIM
    keys, values = block[:, at : at + HEAD_DIM], block[:, kv_cols + at : kv_cols + at + HEAD_DIM]
    scores = lax.dot_general(
        stacked(q_ref, heads), keys, (((1,), (1,)), ((), ())), preferred_element_type=jnp.float32
    )
    scores = scores.reshape(len(heads), *bias.shape) + bias[None]
    ones = jnp.ones_like(values)
    return scores.reshape(-1, bias.shape[1]), jnp.concatenate([values, ones], axis=1)


def weigh(scores, row_max, values):
    rounded = jnp.exp2((scores - row_max) * EXP2_SCALE).astype(jnp.bfloat16)
    summed = jnp.dot(rounded, values, preferred_element_type=jnp.float32)
    return summed[:, :HEAD_DIM], summed[:, HEAD_DIM:]


def near_kernel(q_ref, bias_ref, own_ref, peer_ref, near_ref, far_ref, max_ref, sum_ref, out_ref):
    stretch_part, kv_cols = near_ref.shape[0], own_ref.shape[1] // 2
    all_cols = near_ref.shape[1] // 2
    at = [0, all_cols]
    if all_cols != kv_cols:
        at = [pl.multiple_of(lax.axis_index("sub") * kv_cols + x, HEAD_DIM) for x in at]
    near = jnp.concatenate([near_ref[:, pl.ds(x, kv_cols)] for x in at], axis=1)
    block = jnp.concatenate(
        [own_ref[:stretch_part], peer_ref[:stretch_part], near, far_ref[...]], axis=0
    )
    tok_rows, head_cols = q_ref.shape
    per_group = head_cols // kv_cols
    bias = bias_ref[:, : block.shape[0]]
    for first in range(0, head_cols // HEAD_DIM, HEADS_AT_ONCE):
        heads = range(first, min(first + HEADS_AT_ONCE, head_cols // HEAD_DIM))
        scores, values = attend(q_ref, bias, block, first // per_group, heads)
        row_max = jnp.max(scores, axis=1, keepdims=True)
        weighted, row_sum = weigh(scores, row_max, values)
        row_max = jnp.broadcast_to(row_max, weighted.shape)
        for i, head in enumerate(heads):
            here, rows = pl.ds(head * HEAD_DIM, HEAD_DIM), slice(i * tok_rows, (i + 1) * tok_rows)
            max_ref[:, here] = row_max[rows]
            sum_ref[:, here] = row_sum[rows]
            out_ref[:, here] = weighted[rows]


def later_kernel(picks, q_ref, bias_ref, max_ref, sum_ref, weighted_ref, *refs):
    later_refs, (o_ref, out, sem) = refs[:-3], refs[-3:]
    ctx_pos, sub_pos = lax.axis_index("ctx"), lax.axis_index("sub")
    tok_rows, head_cols = q_ref.shape
    blocks = [None] * (bias_ref.shape[1] // tok_rows)
    for later_ref, pick in zip(later_refs, picks):
        for slot in sorted({slot for _, _, slot in pick}):
            here = [(ctx_pos == dest) & (sub_pos == sub) for dest, sub, at in pick if at == slot]
            block = later_ref[...]
            if blocks[slot] is not None:
                block = jnp.where(functools.reduce(jnp.logical_or, here), block, blocks[slot])
            blocks[slot] = block
    block = jnp.concatenate(blocks[2:], axis=0)
    per_group = head_cols // (block.shape[1] // 2)
    bias = bias_ref[:, 2 * tok_rows :]
    head_count = head_cols // HEAD_DIM
    batches = [
        range(first, min(first + LATER_HEADS, head_count))
        for first in range(0, head_count, LATER_HEADS)
    ]
    attended = [attend(q_ref, bias, block, heads[0] // per_group, heads) for heads in batches]
    for heads, (scores, values) in zip(batches, attended):
        old_max = stacked(max_ref, heads)
        row_max = jnp.maximum(old_max, jnp.max(scores, axis=1, keepdims=True))
        wide_max = jnp.concatenate([row_max] * (block.shape[0] // HEAD_DIM), axis=1)
        weighted, row_sum = weigh(scores, wide_max, values)
        shrink = jnp.exp2((old_max - row_max) * EXP2_SCALE)
        weighted = stacked(weighted_ref, heads) * shrink + weighted
        row_sum = stacked(sum_ref, heads) * shrink + row_sum
        result = (weighted * pl.reciprocal(row_sum, approx=True)).astype(out.dtype)
        for i, head in enumerate(heads):
            here = pl.ds(head * HEAD_DIM, HEAD_DIM)
            out[:, here] = result[i * tok_rows : (i + 1) * tok_rows]
        here = pl.ds(heads[0] * HEAD_DIM, len(heads) * HEAD_DIM)
        pltpu.make_async_copy(out.at[:, here], o_ref.at[:, here], sem).start()
    pltpu.make_async_copy(out, o_ref, sem).wait()


def plan_rounds(n_ctx, n_sub, reach, tok_rows, cache_part, shard_rows):
    per_shard = shard_rows // tok_rows
    cached, stretch = [], []
    for dest in range(n_ctx):
        for slot in range(2, reach + 1):
            back = slot - dest
            if back <= 0:
                stretch.append((dest - slot, None, dest, slot))
                continue
            source = n_ctx - 1 - (back - 1) // per_shard
            row = shard_rows - ((back - 1) % per_shard + 1) * tok_rows
            if dest == 0 and back == 2:
                row = cache_part
            cached.append((source, row, dest, slot))
    rounds = []
    for source, row, dest, slot in cached + stretch:
        for sub in range(n_sub):
            dests = [{(d, i) for (_, i), (_, d, _) in step.items()} for step in rounds]
            free = [
                i for i, step in enumerate(rounds)
                if (source, sub) not in step and (dest, sub) not in dests[i]
            ]
            free.sort(key=lambda i: ((source, sub) in dests[i]) == (sub > 0))
            if not free:
                rounds.append({})
                free = [len(rounds) - 1]
            rounds[free[0]][source, sub] = (row, dest, slot)
    return rounds


def on_device(queries, stretch_keys, stretch_values, cache_keys, cache_values, doc_lengths):
    n_ctx = lax.axis_size("ctx")
    n_sub = lax.axis_size("sub")
    ctx_pos = lax.axis_index("ctx")
    sub_pos = lax.axis_index("sub")
    tok_rows = queries.shape[0]
    stretch_part, all_cols = stretch_keys.shape
    cache_part = cache_keys.shape[0]
    prefix_len = cache_part * n_sub * n_ctx
    head_cols = queries.shape[1] // n_sub
    reach = n_ctx // 2
    assert cache_part == 3 * stretch_part and tok_rows == 2 * stretch_part
    kv_cols = all_cols // n_sub if all_cols // HEAD_DIM % n_sub == 0 else all_cols
    vmem = pl.BlockSpec(memory_space=pltpu.VMEM)
    hbm = pl.BlockSpec(memory_space=pltpu.HBM)
    small = pltpu.CompilerParams(vmem_limit_bytes=8 << 20)

    def in_hbm(*arrays):
        return [pltpu.with_memory_space_constraint(x, pltpu.HBM) for x in arrays]

    rounds = plan_rounds(n_ctx, n_sub, reach, tok_rows, cache_part, cache_part * n_sub)
    owners = {
        (source, row // cache_part)
        for step in rounds
        for (source, _), (first, _, _) in step.items()
        if first is not None
        for row in (first, first + tok_rows - 1)
    }
    half = jax.ShapeDtypeStruct((stretch_part + cache_part, 2 * kv_cols), stretch_keys.dtype)
    raw, mine, theirs = pl.pallas_call(
        functools.partial(pack_kernel, n_ctx, sorted(owners)),
        out_shape=[
            jax.ShapeDtypeStruct((stretch_part, 2 * all_cols), stretch_keys.dtype), half, half
        ],
        in_specs=[hbm] * 4,
        out_specs=[vmem] * 3,
        scratch_shapes=[pltpu.SemaphoreType.DMA((3,))],
        compiler_params=small,
    )(*in_hbm(stretch_keys, stretch_values, cache_keys, cache_values))
    bias = pl.pallas_call(
        functools.partial(bias_kernel, prefix_len, stretch_part, cache_part),
        out_shape=jax.ShapeDtypeStruct((tok_rows, (reach + 1) * tok_rows), jnp.float32),
        in_specs=[hbm],
        out_specs=vmem,
        scratch_shapes=[pltpu.SMEM(doc_lengths.shape, jnp.int32), pltpu.SemaphoreType.DMA],
        compiler_params=small,
    )(*in_hbm(doc_lengths))

    peers = swap_cores(theirs)
    near = lax.ppermute(raw, "ctx", [(i, (i + 1) % n_ctx) for i in range(n_ctx)])

    def cached_rows(row):
        parts = []
        for owner in range(n_sub):
            low = max(row, owner * cache_part) - owner * cache_part + stretch_part
            high = min(row + tok_rows, (owner + 1) * cache_part) - owner * cache_part + stretch_part
            if low < high:
                parts.append(jnp.where(sub_pos == owner, mine[low:high], peers[low:high]))
        return jnp.concatenate(parts) if len(parts) > 1 else parts[0]

    own = jnp.concatenate([mine[:stretch_part], peers[:stretch_part]])
    sent, later, picks = [], [], []
    for step in rounds:
        block = own
        for source, row in sorted({(src, leg[0]) for (src, _), leg in step.items() if leg[0] is not None}):
            block = jnp.where(ctx_pos == source, cached_rows(row), block)
        pairs = [(src * n_sub + sub, leg[1] * n_sub + sub) for (src, sub), leg in step.items()]
        sent.append(block)
        later.append(lax.ppermute(block, ("ctx", "sub"), pairs))
        picks.append([(dest, sub, slot) for (_, sub), (_, dest, slot) in step.items()])

    near, *_ = lax.optimization_barrier((near, *sent[::-1]))
    if kv_cols != all_cols:
        at = (1 - sub_pos) * kv_cols
        near_theirs = jnp.concatenate(
            [
                lax.dynamic_slice_in_dim(near, at, kv_cols, 1),
                lax.dynamic_slice_in_dim(near, at + all_cols, kv_cols, 1),
            ],
            axis=1,
        )
    else:
        near_theirs = near
    far = swap_cores(near_theirs)
    mine_q = lax.dynamic_slice_in_dim(queries, sub_pos * head_cols, head_cols, 1)
    state = jax.ShapeDtypeStruct((tok_rows, head_cols), jnp.float32)
    large = pltpu.CompilerParams(vmem_limit_bytes=24 << 20)
    row_max, row_sum, weighted = pl.pallas_call(
        near_kernel,
        out_shape=[state] * 3,
        in_specs=[vmem] * 6,
        out_specs=[vmem] * 3,
        compiler_params=large,
    )(mine_q, bias, mine, peers, near, far)
    return pl.pallas_call(
        functools.partial(later_kernel, picks),
        out_shape=jax.ShapeDtypeStruct((tok_rows, head_cols), queries.dtype),
        in_specs=[vmem] * (5 + len(later)),
        out_specs=hbm,
        scratch_shapes=[
            pltpu.VMEM((tok_rows, head_cols), queries.dtype),
            pltpu.SemaphoreType.DMA,
        ],
        compiler_params=large,
    )(mine_q, bias, row_max, row_sum, weighted, *later)


def solution(mesh):
    in_specs = (
        P(("grp", "ctx"), "head"),
        P(("grp", "ctx", "sub"), "head"),
        P(("grp", "ctx", "sub"), "head"),
        P(("grp", "ctx", "sub"), "head"),
        P(("grp", "ctx", "sub"), "head"),
        P("grp"),
    )
    out_specs = P(("grp", "ctx"), ("head", "sub"))
    return jax.shard_map(
        on_device, mesh=mesh, in_specs=in_specs, out_specs=out_specs, check_vma=False
    )
```

```python
import functools
import math

import jax
import jax.numpy as jnp
from jax import lax
from jax.experimental import pallas as pl
from jax.experimental.pallas import tpu as pltpu
from jax.sharding import PartitionSpec as P

HEAD_DIM = 128
NEG_FILL = -1e30
SCORE_SCALE = HEAD_DIM ** (-0.5)
EXP2_SCALE = SCORE_SCALE * math.log2(math.e)
HEADS_AT_ONCE = 8
LATER_HEADS = 2


def swap_cores(x):
    return lax.ppermute(x, "sub", [(0, 1), (1, 0)])


def pack_kernel(n_ctx, owners, k_ref, v_ref, ck_ref, cv_ref, raw_ref, mine_ref, theirs_ref, sems):
    ctx_pos, sub_pos = lax.axis_index("ctx"), lax.axis_index("sub")
    last = ctx_pos == n_ctx - 1
    owns = functools.reduce(jnp.logical_or, [(ctx_pos == c) & (sub_pos == s) for c, s in owners])
    stretch_part, all_cols = k_ref.shape
    cache_part = ck_ref.shape[0]
    kv_cols = mine_ref.shape[1] // 2
    for i, (own_src, cache_src) in enumerate([(k_ref, ck_ref), (v_ref, cv_ref)]):
        dst = raw_ref.at[:, pl.ds(i * all_cols, all_cols)]
        from_own = pltpu.make_async_copy(own_src, dst, sems.at[0])
        tail = cache_src.at[pl.ds(cache_part - stretch_part, stretch_part), :]
        from_cache = pltpu.make_async_copy(tail, dst, sems.at[0])
        pl.when(last)(from_cache.start)
        pl.when(jnp.logical_not(last))(from_own.start)
    cached = pl.ds(stretch_part, cache_part)
    for n, (dst, owner) in enumerate([(theirs_ref, 1 - sub_pos), (mine_ref, sub_pos)]):
        at = pl.multiple_of(owner * kv_cols, HEAD_DIM) if kv_cols != all_cols else 0
        for src, rows, col, sem in [
            (k_ref, pl.ds(0, stretch_part), 0, 0),
            (v_ref, pl.ds(0, stretch_part), kv_cols, 0),
            (ck_ref, cached, 0, 1 + n),
            (cv_ref, cached, kv_cols, 1 + n),
        ]:
            part = src.at[:, pl.ds(at, kv_cols)]
            copy = pltpu.make_async_copy(part, dst.at[rows, pl.ds(col, kv_cols)], sems.at[sem])
            if sem:
                pl.when(owns)(copy.start)
            else:
                copy.start()

    def wait_for(rows, sem):
        pltpu.make_async_copy(mine_ref.at[rows, :], mine_ref.at[rows, :], sems.at[sem]).wait()

    @pl.when(owns)
    def _():
        wait_for(cached, 1)
        wait_for(cached, 2)

    wait_for(pl.ds(0, stretch_part * (all_cols + 2 * kv_cols) // kv_cols), 0)


def bias_kernel(prefix_len, stretch_part, cache_part, len_ref, bias_ref, lengths, sem):
    copy = pltpu.make_async_copy(len_ref, lengths, sem)
    copy.start()
    sub_pos, ctx_pos = lax.axis_index("sub"), lax.axis_index("ctx")
    tok_rows = bias_ref.shape[0]
    n_sub = tok_rows // stretch_part
    first = prefix_len + ctx_pos * tok_rows
    row = lax.broadcasted_iota(jnp.int32, (tok_rows, tok_rows), 0)
    lane = lax.broadcasted_iota(jnp.int32, (tok_rows, tok_rows), 1)
    doc_start = jnp.zeros((tok_rows, tok_rows), jnp.int32)
    copy.wait()
    end = jnp.int32(0)
    for doc in range(lengths.shape[0]):
        end = end + lengths[doc]
        doc_start = jnp.where(first + row >= end, end, doc_start)
    for slot in range(bias_ref.shape[1] // tok_rows):
        at = first - slot * tok_rows
        low, high = at + sub_pos * stretch_part, at + (1 - sub_pos) * stretch_part
        if slot == 1:
            tail = prefix_len - (n_sub - 1) * cache_part - stretch_part
            low = jnp.where(ctx_pos == 0, tail + sub_pos * cache_part, low)
            high = jnp.where(ctx_pos == 0, tail + (1 - sub_pos) * cache_part, high)
        elif slot > 1:
            at = jnp.where(ctx_pos == 0, prefix_len - cache_part, at) if slot == 2 else at
            low = jnp.where(ctx_pos < slot, at, low)
            high = jnp.where(ctx_pos < slot, at + stretch_part, high)
        key = jnp.where(lane < stretch_part, low + lane, high + lane - stretch_part)
        allowed = key >= doc_start
        if slot == 0:
            allowed = allowed & (key <= first + row)
        bias_ref[:, slot * tok_rows : (slot + 1) * tok_rows] = jnp.where(allowed, 0.0, NEG_FILL)


def stacked(ref, heads):
    return jnp.concatenate([ref[:, h * HEAD_DIM : (h + 1) * HEAD_DIM] for h in heads], axis=0)


def attend(q_ref, bias, block, group, heads):
    kv_cols = block.shape[1] // 2
    at = group * HEAD_DIM
    keys, values = block[:, at : at + HEAD_DIM], block[:, kv_cols + at : kv_cols + at + HEAD_DIM]
    scores = lax.dot_general(
        stacked(q_ref, heads), keys, (((1,), (1,)), ((), ())), preferred_element_type=jnp.float32
    )
    scores = scores.reshape(len(heads), *bias.shape) + bias[None]
    ones = jnp.ones_like(values)
    return scores.reshape(-1, bias.shape[1]), jnp.concatenate([values, ones], axis=1)


def weigh(scores, row_max, values):
    rounded = jnp.exp2((scores - row_max) * EXP2_SCALE).astype(jnp.bfloat16)
    summed = jnp.dot(rounded, values, preferred_element_type=jnp.float32)
    return summed[:, :HEAD_DIM], summed[:, HEAD_DIM:]


def near_kernel(q_ref, bias_ref, own_ref, peer_ref, near_ref, far_ref, max_ref, sum_ref, out_ref):
    stretch_part, kv_cols = near_ref.shape[0], own_ref.shape[1] // 2
    all_cols = near_ref.shape[1] // 2
    at = [0, all_cols]
    if all_cols != kv_cols:
        at = [pl.multiple_of(lax.axis_index("sub") * kv_cols + x, HEAD_DIM) for x in at]
    near = jnp.concatenate([near_ref[:, pl.ds(x, kv_cols)] for x in at], axis=1)
    block = jnp.concatenate(
        [own_ref[:stretch_part], peer_ref[:stretch_part], near, far_ref[...]], axis=0
    )
    tok_rows, head_cols = q_ref.shape
    per_group = head_cols // kv_cols
    bias = bias_ref[:, : block.shape[0]]
    for first in range(0, head_cols // HEAD_DIM, HEADS_AT_ONCE):
        heads = range(first, min(first + HEADS_AT_ONCE, head_cols // HEAD_DIM))
        scores, values = attend(q_ref, bias, block, first // per_group, heads)
        row_max = jnp.max(scores, axis=1, keepdims=True)
        weighted, row_sum = weigh(scores, row_max, values)
        row_max = jnp.broadcast_to(row_max, weighted.shape)
        for i, head in enumerate(heads):
            here, rows = pl.ds(head * HEAD_DIM, HEAD_DIM), slice(i * tok_rows, (i + 1) * tok_rows)
            max_ref[:, here] = row_max[rows]
            sum_ref[:, here] = row_sum[rows]
            out_ref[:, here] = weighted[rows]


def later_kernel(picks, q_ref, bias_ref, max_ref, sum_ref, weighted_ref, *refs):
    later_refs, (o_ref, out, sem) = refs[:-3], refs[-3:]
    ctx_pos, sub_pos = lax.axis_index("ctx"), lax.axis_index("sub")
    tok_rows, head_cols = q_ref.shape
    blocks = [None] * (bias_ref.shape[1] // tok_rows)
    for later_ref, pick in zip(later_refs, picks):
        for slot in sorted({slot for _, _, slot in pick}):
            here = [(ctx_pos == dest) & (sub_pos == sub) for dest, sub, at in pick if at == slot]
            block = later_ref[...]
            if blocks[slot] is not None:
                block = jnp.where(functools.reduce(jnp.logical_or, here), block, blocks[slot])
            blocks[slot] = block
    block = jnp.concatenate(blocks[2:], axis=0)
    per_group = head_cols // (block.shape[1] // 2)
    bias = bias_ref[:, 2 * tok_rows :]
    head_count = head_cols // HEAD_DIM
    batches = [
        range(first, min(first + LATER_HEADS, head_count))
        for first in range(0, head_count, LATER_HEADS)
    ]
    attended = [attend(q_ref, bias, block, heads[0] // per_group, heads) for heads in batches]
    for heads, (scores, values) in zip(batches, attended):
        old_max = stacked(max_ref, heads)
        row_max = jnp.maximum(old_max, jnp.max(scores, axis=1, keepdims=True))
        wide_max = jnp.concatenate([row_max] * (block.shape[0] // HEAD_DIM), axis=1)
        weighted, row_sum = weigh(scores, wide_max, values)
        shrink = jnp.exp2((old_max - row_max) * EXP2_SCALE)
        weighted = stacked(weighted_ref, heads) * shrink + weighted
        row_sum = stacked(sum_ref, heads) * shrink + row_sum
        result = (weighted * pl.reciprocal(row_sum, approx=True)).astype(out.dtype)
        for i, head in enumerate(heads):
            here = pl.ds(head * HEAD_DIM, HEAD_DIM)
            out[:, here] = result[i * tok_rows : (i + 1) * tok_rows]
        here = pl.ds(heads[0] * HEAD_DIM, len(heads) * HEAD_DIM)
        pltpu.make_async_copy(out.at[:, here], o_ref.at[:, here], sem).start()
    pltpu.make_async_copy(out, o_ref, sem).wait()


def plan_rounds(n_ctx, n_sub, reach, tok_rows, cache_part, shard_rows):
    per_shard = shard_rows // tok_rows
    cached, stretch = [], []
    for dest in range(n_ctx):
        for slot in range(2, reach + 1):
            back = slot - dest
            if back <= 0:
                stretch.append((dest - slot, None, dest, slot))
                continue
            source = n_ctx - 1 - (back - 1) // per_shard
            row = shard_rows - ((back - 1) % per_shard + 1) * tok_rows
            if dest == 0 and back == 2:
                row = cache_part
            cached.append((source, row, dest, slot))
    rounds = []
    for source, row, dest, slot in cached + stretch:
        for sub in range(n_sub):
            dests = [{(d, i) for (_, i), (_, d, _) in step.items()} for step in rounds]
            free = [
                i for i, step in enumerate(rounds)
                if (source, sub) not in step and (dest, sub) not in dests[i]
            ]
            if sub == 0:
                free.sort(key=lambda i: (source, sub) not in dests[i])
            if not free:
                rounds.append({})
                free = [len(rounds) - 1]
            rounds[free[0]][source, sub] = (row, dest, slot)
    return rounds


def on_device(queries, stretch_keys, stretch_values, cache_keys, cache_values, doc_lengths):
    n_ctx = lax.axis_size("ctx")
    n_sub = lax.axis_size("sub")
    ctx_pos = lax.axis_index("ctx")
    sub_pos = lax.axis_index("sub")
    tok_rows = queries.shape[0]
    stretch_part, all_cols = stretch_keys.shape
    cache_part = cache_keys.shape[0]
    prefix_len = cache_part * n_sub * n_ctx
    head_cols = queries.shape[1] // n_sub
    reach = n_ctx // 2
    assert cache_part == 3 * stretch_part and tok_rows == 2 * stretch_part
    kv_cols = all_cols // n_sub if all_cols // HEAD_DIM % n_sub == 0 else all_cols
    vmem = pl.BlockSpec(memory_space=pltpu.VMEM)
    hbm = pl.BlockSpec(memory_space=pltpu.HBM)
    small = pltpu.CompilerParams(vmem_limit_bytes=8 << 20)

    def in_hbm(*arrays):
        return [pltpu.with_memory_space_constraint(x, pltpu.HBM) for x in arrays]

    rounds = plan_rounds(n_ctx, n_sub, reach, tok_rows, cache_part, cache_part * n_sub)
    owners = {
        (source, row // cache_part)
        for step in rounds
        for (source, _), (first, _, _) in step.items()
        if first is not None
        for row in (first, first + tok_rows - 1)
    }
    half = jax.ShapeDtypeStruct((stretch_part + cache_part, 2 * kv_cols), stretch_keys.dtype)
    raw, mine, theirs = pl.pallas_call(
        functools.partial(pack_kernel, n_ctx, sorted(owners)),
        out_shape=[
            jax.ShapeDtypeStruct((stretch_part, 2 * all_cols), stretch_keys.dtype), half, half
        ],
        in_specs=[hbm] * 4,
        out_specs=[vmem] * 3,
        scratch_shapes=[pltpu.SemaphoreType.DMA((3,))],
        compiler_params=small,
    )(*in_hbm(stretch_keys, stretch_values, cache_keys, cache_values))
    bias = pl.pallas_call(
        functools.partial(bias_kernel, prefix_len, stretch_part, cache_part),
        out_shape=jax.ShapeDtypeStruct((tok_rows, (reach + 1) * tok_rows), jnp.float32),
        in_specs=[hbm],
        out_specs=vmem,
        scratch_shapes=[pltpu.SMEM(doc_lengths.shape, jnp.int32), pltpu.SemaphoreType.DMA],
        compiler_params=small,
    )(*in_hbm(doc_lengths))

    peers = swap_cores(theirs)
    near = lax.ppermute(raw, "ctx", [(i, (i + 1) % n_ctx) for i in range(n_ctx)])

    def cached_rows(row):
        parts = []
        for owner in range(n_sub):
            low = max(row, owner * cache_part) - owner * cache_part + stretch_part
            high = min(row + tok_rows, (owner + 1) * cache_part) - owner * cache_part + stretch_part
            if low < high:
                parts.append(jnp.where(sub_pos == owner, mine[low:high], peers[low:high]))
        return jnp.concatenate(parts) if len(parts) > 1 else parts[0]

    own = jnp.concatenate([mine[:stretch_part], peers[:stretch_part]])
    sent, later, picks = [], [], []
    for step in rounds:
        block = own
        for source, row in sorted({(src, leg[0]) for (src, _), leg in step.items() if leg[0] is not None}):
            block = jnp.where(ctx_pos == source, cached_rows(row), block)
        pairs = [(src * n_sub + sub, leg[1] * n_sub + sub) for (src, sub), leg in step.items()]
        sent.append(block)
        later.append(lax.ppermute(block, ("ctx", "sub"), pairs))
        picks.append([(dest, sub, slot) for (_, sub), (_, dest, slot) in step.items()])

    near, *_ = lax.optimization_barrier((near, *sent[::-1]))
    if kv_cols != all_cols:
        at = (1 - sub_pos) * kv_cols
        near_theirs = jnp.concatenate(
            [
                lax.dynamic_slice_in_dim(near, at, kv_cols, 1),
                lax.dynamic_slice_in_dim(near, at + all_cols, kv_cols, 1),
            ],
            axis=1,
        )
    else:
        near_theirs = near
    far = swap_cores(near_theirs)
    mine_q = lax.dynamic_slice_in_dim(queries, sub_pos * head_cols, head_cols, 1)
    state = jax.ShapeDtypeStruct((tok_rows, head_cols), jnp.float32)
    large = pltpu.CompilerParams(vmem_limit_bytes=24 << 20)
    row_max, row_sum, weighted = pl.pallas_call(
        near_kernel,
        out_shape=[state] * 3,
        in_specs=[vmem] * 6,
        out_specs=[vmem] * 3,
        compiler_params=large,
    )(mine_q, bias, mine, peers, near, far)
    return pl.pallas_call(
        functools.partial(later_kernel, picks),
        out_shape=jax.ShapeDtypeStruct((tok_rows, head_cols), queries.dtype),
        in_specs=[vmem] * (5 + len(later)),
        out_specs=hbm,
        scratch_shapes=[
            pltpu.VMEM((tok_rows, head_cols), queries.dtype),
            pltpu.SemaphoreType.DMA,
        ],
        compiler_params=large,
    )(mine_q, bias, row_max, row_sum, weighted, *later)


def solution(mesh):
    in_specs = (
        P(("grp", "ctx"), "head"),
        P(("grp", "ctx", "sub"), "head"),
        P(("grp", "ctx", "sub"), "head"),
        P(("grp", "ctx", "sub"), "head"),
        P(("grp", "ctx", "sub"), "head"),
        P("grp"),
    )
    out_specs = P(("grp", "ctx"), ("head", "sub"))
    return jax.shard_map(
        on_device, mesh=mesh, in_specs=in_specs, out_specs=out_specs, check_vma=False
    )
```

```python
import functools
import math

import jax
import jax.numpy as jnp
from jax import lax
from jax.experimental import pallas as pl
from jax.experimental.pallas import tpu as pltpu
from jax.sharding import PartitionSpec as P

HEAD_DIM = 128
NEG_FILL = -1e30
SCORE_SCALE = HEAD_DIM ** (-0.5)
EXP2_SCALE = SCORE_SCALE * math.log2(math.e)
HEADS_AT_ONCE = 8
LATER_HEADS = 2
HEADS_PER_COPY = 4


def swap_cores(x):
    return lax.ppermute(x, "sub", [(0, 1), (1, 0)])


def pack_kernel(n_ctx, owners, k_ref, v_ref, ck_ref, cv_ref, raw_ref, mine_ref, theirs_ref, sems):
    ctx_pos, sub_pos = lax.axis_index("ctx"), lax.axis_index("sub")
    last = ctx_pos == n_ctx - 1
    owns = functools.reduce(jnp.logical_or, [(ctx_pos == c) & (sub_pos == s) for c, s in owners])
    stretch_part, all_cols = k_ref.shape
    cache_part = ck_ref.shape[0]
    kv_cols = mine_ref.shape[1] // 2
    for i, (own_src, cache_src) in enumerate([(k_ref, ck_ref), (v_ref, cv_ref)]):
        dst = raw_ref.at[:, pl.ds(i * all_cols, all_cols)]
        from_own = pltpu.make_async_copy(own_src, dst, sems.at[0])
        tail = cache_src.at[pl.ds(cache_part - stretch_part, stretch_part), :]
        from_cache = pltpu.make_async_copy(tail, dst, sems.at[0])
        pl.when(last)(from_cache.start)
        pl.when(jnp.logical_not(last))(from_own.start)
    cached = pl.ds(stretch_part, cache_part)
    for n, (dst, owner) in enumerate([(theirs_ref, 1 - sub_pos), (mine_ref, sub_pos)]):
        at = pl.multiple_of(owner * kv_cols, HEAD_DIM) if kv_cols != all_cols else 0
        for src, rows, col, sem in [
            (k_ref, pl.ds(0, stretch_part), 0, 0),
            (v_ref, pl.ds(0, stretch_part), kv_cols, 0),
            (ck_ref, cached, 0, 1 + n),
            (cv_ref, cached, kv_cols, 1 + n),
        ]:
            part = src.at[:, pl.ds(at, kv_cols)]
            copy = pltpu.make_async_copy(part, dst.at[rows, pl.ds(col, kv_cols)], sems.at[sem])
            if sem:
                pl.when(owns)(copy.start)
            else:
                copy.start()

    def wait_for(rows, sem):
        pltpu.make_async_copy(mine_ref.at[rows, :], mine_ref.at[rows, :], sems.at[sem]).wait()

    @pl.when(owns)
    def _():
        wait_for(cached, 1)
        wait_for(cached, 2)

    wait_for(pl.ds(0, stretch_part * (all_cols + 2 * kv_cols) // kv_cols), 0)


def bias_kernel(prefix_len, stretch_part, cache_part, len_ref, bias_ref, lengths, sem):
    copy = pltpu.make_async_copy(len_ref, lengths, sem)
    copy.start()
    sub_pos, ctx_pos = lax.axis_index("sub"), lax.axis_index("ctx")
    tok_rows = bias_ref.shape[0]
    n_sub = tok_rows // stretch_part
    first = prefix_len + ctx_pos * tok_rows
    row = lax.broadcasted_iota(jnp.int32, (tok_rows, tok_rows), 0)
    lane = lax.broadcasted_iota(jnp.int32, (tok_rows, tok_rows), 1)
    doc_start = jnp.zeros((tok_rows, tok_rows), jnp.int32)
    copy.wait()
    end = jnp.int32(0)
    for doc in range(lengths.shape[0]):
        end = end + lengths[doc]
        doc_start = jnp.where(first + row >= end, end, doc_start)
    for slot in range(bias_ref.shape[1] // tok_rows):
        at = first - slot * tok_rows
        low, high = at + sub_pos * stretch_part, at + (1 - sub_pos) * stretch_part
        if slot == 1:
            tail = prefix_len - (n_sub - 1) * cache_part - stretch_part
            low = jnp.where(ctx_pos == 0, tail + sub_pos * cache_part, low)
            high = jnp.where(ctx_pos == 0, tail + (1 - sub_pos) * cache_part, high)
        elif slot > 1:
            at = jnp.where(ctx_pos == 0, prefix_len - cache_part, at) if slot == 2 else at
            low = jnp.where(ctx_pos < slot, at, low)
            high = jnp.where(ctx_pos < slot, at + stretch_part, high)
        key = jnp.where(lane < stretch_part, low + lane, high + lane - stretch_part)
        allowed = key >= doc_start
        if slot == 0:
            allowed = allowed & (key <= first + row)
        bias_ref[:, slot * tok_rows : (slot + 1) * tok_rows] = jnp.where(allowed, 0.0, NEG_FILL)


def stacked(ref, heads):
    return jnp.concatenate([ref[:, h * HEAD_DIM : (h + 1) * HEAD_DIM] for h in heads], axis=0)


def attend(q_ref, bias, block, group, heads):
    kv_cols = block.shape[1] // 2
    at = group * HEAD_DIM
    keys, values = block[:, at : at + HEAD_DIM], block[:, kv_cols + at : kv_cols + at + HEAD_DIM]
    scores = lax.dot_general(
        stacked(q_ref, heads), keys, (((1,), (1,)), ((), ())), preferred_element_type=jnp.float32
    )
    scores = scores.reshape(len(heads), *bias.shape) + bias[None]
    ones = jnp.ones_like(values)
    return scores.reshape(-1, bias.shape[1]), jnp.concatenate([values, ones], axis=1)


def weigh(scores, row_max, values):
    rounded = jnp.exp2((scores - row_max) * EXP2_SCALE).astype(jnp.bfloat16)
    summed = jnp.dot(rounded, values, preferred_element_type=jnp.float32)
    return summed[:, :HEAD_DIM], summed[:, HEAD_DIM:]


def near_kernel(q_ref, bias_ref, own_ref, peer_ref, near_ref, far_ref, max_ref, sum_ref, out_ref):
    stretch_part, kv_cols = near_ref.shape[0], own_ref.shape[1] // 2
    all_cols = near_ref.shape[1] // 2
    at = [0, all_cols]
    if all_cols != kv_cols:
        at = [pl.multiple_of(lax.axis_index("sub") * kv_cols + x, HEAD_DIM) for x in at]
    near = jnp.concatenate([near_ref[:, pl.ds(x, kv_cols)] for x in at], axis=1)
    block = jnp.concatenate(
        [own_ref[:stretch_part], peer_ref[:stretch_part], near, far_ref[...]], axis=0
    )
    tok_rows, head_cols = q_ref.shape
    per_group = head_cols // kv_cols
    bias = bias_ref[:, : block.shape[0]]
    for first in range(0, head_cols // HEAD_DIM, HEADS_AT_ONCE):
        heads = range(first, min(first + HEADS_AT_ONCE, head_cols // HEAD_DIM))
        scores, values = attend(q_ref, bias, block, first // per_group, heads)
        row_max = jnp.max(scores, axis=1, keepdims=True)
        weighted, row_sum = weigh(scores, row_max, values)
        row_max = jnp.broadcast_to(row_max, weighted.shape)
        for i, head in enumerate(heads):
            here, rows = pl.ds(head * HEAD_DIM, HEAD_DIM), slice(i * tok_rows, (i + 1) * tok_rows)
            max_ref[:, here] = row_max[rows]
            sum_ref[:, here] = row_sum[rows]
            out_ref[:, here] = weighted[rows]


def later_kernel(picks, q_ref, bias_ref, max_ref, sum_ref, weighted_ref, *refs):
    later_refs, (o_ref, out, sem) = refs[:-3], refs[-3:]
    ctx_pos, sub_pos = lax.axis_index("ctx"), lax.axis_index("sub")
    tok_rows, head_cols = q_ref.shape
    blocks = [None] * (bias_ref.shape[1] // tok_rows)
    for later_ref, pick in zip(later_refs, picks):
        for slot in sorted({slot for _, _, slot in pick}):
            here = [(ctx_pos == dest) & (sub_pos == sub) for dest, sub, at in pick if at == slot]
            block = later_ref[...]
            if blocks[slot] is not None:
                block = jnp.where(functools.reduce(jnp.logical_or, here), block, blocks[slot])
            blocks[slot] = block
    block = jnp.concatenate(blocks[2:], axis=0)
    per_group = head_cols // (block.shape[1] // 2)
    bias = bias_ref[:, 2 * tok_rows :]
    head_count = head_cols // HEAD_DIM
    batches = [
        range(first, min(first + LATER_HEADS, head_count))
        for first in range(0, head_count, LATER_HEADS)
    ]
    attended = [attend(q_ref, bias, block, heads[0] // per_group, heads) for heads in batches]
    for heads, (scores, values) in zip(batches, attended):
        old_max = stacked(max_ref, heads)
        row_max = jnp.maximum(old_max, jnp.max(scores, axis=1, keepdims=True))
        wide_max = jnp.concatenate([row_max] * (block.shape[0] // HEAD_DIM), axis=1)
        weighted, row_sum = weigh(scores, wide_max, values)
        shrink = jnp.exp2((old_max - row_max) * EXP2_SCALE)
        weighted = stacked(weighted_ref, heads) * shrink + weighted
        row_sum = stacked(sum_ref, heads) * shrink + row_sum
        result = (weighted * pl.reciprocal(row_sum, approx=True)).astype(out.dtype)
        for i, head in enumerate(heads):
            here = pl.ds(head * HEAD_DIM, HEAD_DIM)
            out[:, here] = result[i * tok_rows : (i + 1) * tok_rows]
        done = heads[-1] + 1
        if done % HEADS_PER_COPY == 0 or done == head_count:
            at = (done - 1) // HEADS_PER_COPY * HEADS_PER_COPY
            here = pl.ds(at * HEAD_DIM, (done - at) * HEAD_DIM)
            pltpu.make_async_copy(out.at[:, here], o_ref.at[:, here], sem).start()
    pltpu.make_async_copy(out, o_ref, sem).wait()


def plan_rounds(n_ctx, n_sub, reach, tok_rows, cache_part, shard_rows):
    per_shard = shard_rows // tok_rows
    cached, stretch = [], []
    for dest in range(n_ctx):
        for slot in range(2, reach + 1):
            back = slot - dest
            if back <= 0:
                stretch.append((dest - slot, None, dest, slot))
                continue
            source = n_ctx - 1 - (back - 1) // per_shard
            row = shard_rows - ((back - 1) % per_shard + 1) * tok_rows
            if dest == 0 and back == 2:
                row = cache_part
            cached.append((source, row, dest, slot))
    rounds = []
    for source, row, dest, slot in cached + stretch:
        for sub in range(n_sub):
            dests = [{(d, i) for (_, i), (_, d, _) in step.items()} for step in rounds]
            free = [
                i for i, step in enumerate(rounds)
                if (source, sub) not in step and (dest, sub) not in dests[i]
            ]
            free.sort(key=lambda i: ((source, sub) in dests[i]) == (sub > 0))
            if not free:
                rounds.append({})
                free = [len(rounds) - 1]
            rounds[free[0]][source, sub] = (row, dest, slot)
    return rounds


def on_device(queries, stretch_keys, stretch_values, cache_keys, cache_values, doc_lengths):
    n_ctx = lax.axis_size("ctx")
    n_sub = lax.axis_size("sub")
    ctx_pos = lax.axis_index("ctx")
    sub_pos = lax.axis_index("sub")
    tok_rows = queries.shape[0]
    stretch_part, all_cols = stretch_keys.shape
    cache_part = cache_keys.shape[0]
    prefix_len = cache_part * n_sub * n_ctx
    head_cols = queries.shape[1] // n_sub
    reach = n_ctx // 2
    assert cache_part == 3 * stretch_part and tok_rows == 2 * stretch_part
    kv_cols = all_cols // n_sub if all_cols // HEAD_DIM % n_sub == 0 else all_cols
    vmem = pl.BlockSpec(memory_space=pltpu.VMEM)
    hbm = pl.BlockSpec(memory_space=pltpu.HBM)
    small = pltpu.CompilerParams(vmem_limit_bytes=8 << 20)

    def in_hbm(*arrays):
        return [pltpu.with_memory_space_constraint(x, pltpu.HBM) for x in arrays]

    rounds = plan_rounds(n_ctx, n_sub, reach, tok_rows, cache_part, cache_part * n_sub)
    owners = {
        (source, row // cache_part)
        for step in rounds
        for (source, _), (first, _, _) in step.items()
        if first is not None
        for row in (first, first + tok_rows - 1)
    }
    half = jax.ShapeDtypeStruct((stretch_part + cache_part, 2 * kv_cols), stretch_keys.dtype)
    raw, mine, theirs = pl.pallas_call(
        functools.partial(pack_kernel, n_ctx, sorted(owners)),
        out_shape=[
            jax.ShapeDtypeStruct((stretch_part, 2 * all_cols), stretch_keys.dtype), half, half
        ],
        in_specs=[hbm] * 4,
        out_specs=[vmem] * 3,
        scratch_shapes=[pltpu.SemaphoreType.DMA((3,))],
        compiler_params=small,
    )(*in_hbm(stretch_keys, stretch_values, cache_keys, cache_values))
    bias = pl.pallas_call(
        functools.partial(bias_kernel, prefix_len, stretch_part, cache_part),
        out_shape=jax.ShapeDtypeStruct((tok_rows, (reach + 1) * tok_rows), jnp.float32),
        in_specs=[hbm],
        out_specs=vmem,
        scratch_shapes=[pltpu.SMEM(doc_lengths.shape, jnp.int32), pltpu.SemaphoreType.DMA],
        compiler_params=small,
    )(*in_hbm(doc_lengths))

    peers = swap_cores(theirs)
    near = lax.ppermute(raw, "ctx", [(i, (i + 1) % n_ctx) for i in range(n_ctx)])

    def cached_rows(row):
        parts = []
        for owner in range(n_sub):
            low = max(row, owner * cache_part) - owner * cache_part + stretch_part
            high = min(row + tok_rows, (owner + 1) * cache_part) - owner * cache_part + stretch_part
            if low < high:
                parts.append(jnp.where(sub_pos == owner, mine[low:high], peers[low:high]))
        return jnp.concatenate(parts) if len(parts) > 1 else parts[0]

    own = jnp.concatenate([mine[:stretch_part], peers[:stretch_part]])
    sent, later, picks = [], [], []
    for step in rounds:
        block = own
        for source, row in sorted({(src, leg[0]) for (src, _), leg in step.items() if leg[0] is not None}):
            block = jnp.where(ctx_pos == source, cached_rows(row), block)
        pairs = [(src * n_sub + sub, leg[1] * n_sub + sub) for (src, sub), leg in step.items()]
        sent.append(block)
        later.append(lax.ppermute(block, ("ctx", "sub"), pairs))
        picks.append([(dest, sub, slot) for (_, sub), (_, dest, slot) in step.items()])

    near, *_ = lax.optimization_barrier((near, *sent[::-1]))
    if kv_cols != all_cols:
        at = (1 - sub_pos) * kv_cols
        near_theirs = jnp.concatenate(
            [
                lax.dynamic_slice_in_dim(near, at, kv_cols, 1),
                lax.dynamic_slice_in_dim(near, at + all_cols, kv_cols, 1),
            ],
            axis=1,
        )
    else:
        near_theirs = near
    far = swap_cores(near_theirs)
    mine_q = lax.dynamic_slice_in_dim(queries, sub_pos * head_cols, head_cols, 1)
    state = jax.ShapeDtypeStruct((tok_rows, head_cols), jnp.float32)
    large = pltpu.CompilerParams(vmem_limit_bytes=24 << 20)
    row_max, row_sum, weighted = pl.pallas_call(
        near_kernel,
        out_shape=[state] * 3,
        in_specs=[vmem] * 6,
        out_specs=[vmem] * 3,
        compiler_params=large,
    )(mine_q, bias, mine, peers, near, far)
    return pl.pallas_call(
        functools.partial(later_kernel, picks),
        out_shape=jax.ShapeDtypeStruct((tok_rows, head_cols), queries.dtype),
        in_specs=[vmem] * (5 + len(later)),
        out_specs=hbm,
        scratch_shapes=[
            pltpu.VMEM((tok_rows, head_cols), queries.dtype),
            pltpu.SemaphoreType.DMA,
        ],
        compiler_params=large,
    )(mine_q, bias, row_max, row_sum, weighted, *later)


def solution(mesh):
    in_specs = (
        P(("grp", "ctx"), "head"),
        P(("grp", "ctx", "sub"), "head"),
        P(("grp", "ctx", "sub"), "head"),
        P(("grp", "ctx", "sub"), "head"),
        P(("grp", "ctx", "sub"), "head"),
        P("grp"),
    )
    out_specs = P(("grp", "ctx"), ("head", "sub"))
    return jax.shard_map(
        on_device, mesh=mesh, in_specs=in_specs, out_specs=out_specs, check_vma=False
    )
```

```python
import functools
import math

import jax
import jax.numpy as jnp
from jax import lax
from jax.experimental import pallas as pl
from jax.experimental.pallas import tpu as pltpu
from jax.sharding import PartitionSpec as P

HEAD_DIM = 128
NEG_FILL = -1e30
SCORE_SCALE = HEAD_DIM ** (-0.5)
EXP2_SCALE = SCORE_SCALE * math.log2(math.e)
HEADS_AT_ONCE = 8
LATER_HEADS = 2


def swap_cores(x):
    return lax.ppermute(x, "sub", [(0, 1), (1, 0)])


def pack_kernel(n_ctx, owners, k_ref, v_ref, ck_ref, cv_ref, raw_ref, mine_ref, theirs_ref, sems):
    ctx_pos, sub_pos = lax.axis_index("ctx"), lax.axis_index("sub")
    last = ctx_pos == n_ctx - 1
    owns = functools.reduce(jnp.logical_or, [(ctx_pos == c) & (sub_pos == s) for c, s in owners])
    stretch_part, all_cols = k_ref.shape
    cache_part = ck_ref.shape[0]
    kv_cols = mine_ref.shape[1] // 2
    for i, (own_src, cache_src) in enumerate([(k_ref, ck_ref), (v_ref, cv_ref)]):
        dst = raw_ref.at[:, pl.ds(i * all_cols, all_cols)]
        from_own = pltpu.make_async_copy(own_src, dst, sems.at[0])
        tail = cache_src.at[pl.ds(cache_part - stretch_part, stretch_part), :]
        from_cache = pltpu.make_async_copy(tail, dst, sems.at[0])
        pl.when(last)(from_cache.start)
        pl.when(jnp.logical_not(last))(from_own.start)
    cached = pl.ds(stretch_part, cache_part)
    for n, (dst, owner) in enumerate([(theirs_ref, 1 - sub_pos), (mine_ref, sub_pos)]):
        at = pl.multiple_of(owner * kv_cols, HEAD_DIM) if kv_cols != all_cols else 0
        for src, rows, col, sem in [
            (ck_ref, cached, 0, 1 + n),
            (cv_ref, cached, kv_cols, 1 + n),
            (k_ref, pl.ds(0, stretch_part), 0, 0),
            (v_ref, pl.ds(0, stretch_part), kv_cols, 0),
        ]:
            part = src.at[:, pl.ds(at, kv_cols)]
            copy = pltpu.make_async_copy(part, dst.at[rows, pl.ds(col, kv_cols)], sems.at[sem])
            if sem:
                pl.when(owns)(copy.start)
            else:
                copy.start()

    def wait_for(rows, sem):
        pltpu.make_async_copy(mine_ref.at[rows, :], mine_ref.at[rows, :], sems.at[sem]).wait()

    @pl.when(owns)
    def _():
        wait_for(cached, 1)
        wait_for(cached, 2)

    wait_for(pl.ds(0, stretch_part * (all_cols + 2 * kv_cols) // kv_cols), 0)


def bias_kernel(prefix_len, stretch_part, cache_part, len_ref, bias_ref, lengths, sem):
    copy = pltpu.make_async_copy(len_ref, lengths, sem)
    copy.start()
    sub_pos, ctx_pos = lax.axis_index("sub"), lax.axis_index("ctx")
    tok_rows = bias_ref.shape[0]
    n_sub = tok_rows // stretch_part
    first = prefix_len + ctx_pos * tok_rows
    row = lax.broadcasted_iota(jnp.int32, (tok_rows, tok_rows), 0)
    lane = lax.broadcasted_iota(jnp.int32, (tok_rows, tok_rows), 1)
    doc_start = jnp.zeros((tok_rows, tok_rows), jnp.int32)
    copy.wait()
    end = jnp.int32(0)
    for doc in range(lengths.shape[0]):
        end = end + lengths[doc]
        doc_start = jnp.where(first + row >= end, end, doc_start)
    for slot in range(bias_ref.shape[1] // tok_rows):
        at = first - slot * tok_rows
        low, high = at + sub_pos * stretch_part, at + (1 - sub_pos) * stretch_part
        if slot == 1:
            tail = prefix_len - (n_sub - 1) * cache_part - stretch_part
            low = jnp.where(ctx_pos == 0, tail + sub_pos * cache_part, low)
            high = jnp.where(ctx_pos == 0, tail + (1 - sub_pos) * cache_part, high)
        elif slot > 1:
            at = jnp.where(ctx_pos == 0, prefix_len - cache_part, at) if slot == 2 else at
            low = jnp.where(ctx_pos < slot, at, low)
            high = jnp.where(ctx_pos < slot, at + stretch_part, high)
        key = jnp.where(lane < stretch_part, low + lane, high + lane - stretch_part)
        allowed = key >= doc_start
        if slot == 0:
            allowed = allowed & (key <= first + row)
        bias_ref[:, slot * tok_rows : (slot + 1) * tok_rows] = jnp.where(allowed, 0.0, NEG_FILL)


def stacked(ref, heads):
    return jnp.concatenate([ref[:, h * HEAD_DIM : (h + 1) * HEAD_DIM] for h in heads], axis=0)


def attend(q_ref, bias, block, group, heads):
    kv_cols = block.shape[1] // 2
    at = group * HEAD_DIM
    keys, values = block[:, at : at + HEAD_DIM], block[:, kv_cols + at : kv_cols + at + HEAD_DIM]
    scores = lax.dot_general(
        stacked(q_ref, heads), keys, (((1,), (1,)), ((), ())), preferred_element_type=jnp.float32
    )
    scores = scores.reshape(len(heads), *bias.shape) + bias[None]
    ones = jnp.ones_like(values)
    return scores.reshape(-1, bias.shape[1]), jnp.concatenate([values, ones], axis=1)


def weigh(scores, row_max, values):
    rounded = jnp.exp2((scores - row_max) * EXP2_SCALE).astype(jnp.bfloat16)
    summed = jnp.dot(rounded, values, preferred_element_type=jnp.float32)
    return summed[:, :HEAD_DIM], summed[:, HEAD_DIM:]


def near_kernel(q_ref, bias_ref, own_ref, peer_ref, near_ref, far_ref, max_ref, sum_ref, out_ref):
    stretch_part, kv_cols = near_ref.shape[0], own_ref.shape[1] // 2
    all_cols = near_ref.shape[1] // 2
    at = [0, all_cols]
    if all_cols != kv_cols:
        at = [pl.multiple_of(lax.axis_index("sub") * kv_cols + x, HEAD_DIM) for x in at]
    near = jnp.concatenate([near_ref[:, pl.ds(x, kv_cols)] for x in at], axis=1)
    block = jnp.concatenate(
        [own_ref[:stretch_part], peer_ref[:stretch_part], near, far_ref[...]], axis=0
    )
    tok_rows, head_cols = q_ref.shape
    per_group = head_cols // kv_cols
    bias = bias_ref[:, : block.shape[0]]
    for first in range(0, head_cols // HEAD_DIM, HEADS_AT_ONCE):
        heads = range(first, min(first + HEADS_AT_ONCE, head_cols // HEAD_DIM))
        scores, values = attend(q_ref, bias, block, first // per_group, heads)
        row_max = jnp.max(scores, axis=1, keepdims=True)
        weighted, row_sum = weigh(scores, row_max, values)
        row_max = jnp.broadcast_to(row_max, weighted.shape)
        for i, head in enumerate(heads):
            here, rows = pl.ds(head * HEAD_DIM, HEAD_DIM), slice(i * tok_rows, (i + 1) * tok_rows)
            max_ref[:, here] = row_max[rows]
            sum_ref[:, here] = row_sum[rows]
            out_ref[:, here] = weighted[rows]


def later_kernel(picks, q_ref, bias_ref, max_ref, sum_ref, weighted_ref, *refs):
    later_refs, (o_ref, out, sem) = refs[:-3], refs[-3:]
    ctx_pos, sub_pos = lax.axis_index("ctx"), lax.axis_index("sub")
    tok_rows, head_cols = q_ref.shape
    blocks = [None] * (bias_ref.shape[1] // tok_rows)
    for later_ref, pick in zip(later_refs, picks):
        for slot in sorted({slot for _, _, slot in pick}):
            here = [(ctx_pos == dest) & (sub_pos == sub) for dest, sub, at in pick if at == slot]
            block = later_ref[...]
            if blocks[slot] is not None:
                block = jnp.where(functools.reduce(jnp.logical_or, here), block, blocks[slot])
            blocks[slot] = block
    block = jnp.concatenate(blocks[2:], axis=0)
    per_group = head_cols // (block.shape[1] // 2)
    bias = bias_ref[:, 2 * tok_rows :]
    head_count = head_cols // HEAD_DIM
    batches = [
        range(first, min(first + LATER_HEADS, head_count))
        for first in range(0, head_count, LATER_HEADS)
    ]
    attended = [attend(q_ref, bias, block, heads[0] // per_group, heads) for heads in batches]
    for heads, (scores, values) in zip(batches, attended):
        old_max = stacked(max_ref, heads)
        row_max = jnp.maximum(old_max, jnp.max(scores, axis=1, keepdims=True))
        wide_max = jnp.concatenate([row_max] * (block.shape[0] // HEAD_DIM), axis=1)
        weighted, row_sum = weigh(scores, wide_max, values)
        shrink = jnp.exp2((old_max - row_max) * EXP2_SCALE)
        weighted = stacked(weighted_ref, heads) * shrink + weighted
        row_sum = stacked(sum_ref, heads) * shrink + row_sum
        result = (weighted * pl.reciprocal(row_sum, approx=True)).astype(out.dtype)
        for i, head in enumerate(heads):
            here = pl.ds(head * HEAD_DIM, HEAD_DIM)
            out[:, here] = result[i * tok_rows : (i + 1) * tok_rows]
        here = pl.ds(heads[0] * HEAD_DIM, len(heads) * HEAD_DIM)
        pltpu.make_async_copy(out.at[:, here], o_ref.at[:, here], sem).start()
    pltpu.make_async_copy(out, o_ref, sem).wait()


def plan_rounds(n_ctx, n_sub, reach, tok_rows, cache_part, shard_rows):
    per_shard = shard_rows // tok_rows
    cached, stretch = [], []
    for dest in range(n_ctx):
        for slot in range(2, reach + 1):
            back = slot - dest
            if back <= 0:
                stretch.append((dest - slot, None, dest, slot))
                continue
            source = n_ctx - 1 - (back - 1) // per_shard
            row = shard_rows - ((back - 1) % per_shard + 1) * tok_rows
            if dest == 0 and back == 2:
                row = cache_part
            cached.append((source, row, dest, slot))
    rounds = []
    for source, row, dest, slot in cached + stretch:
        for sub in range(n_sub):
            dests = [{(d, i) for (_, i), (_, d, _) in step.items()} for step in rounds]
            free = [
                i for i, step in enumerate(rounds)
                if (source, sub) not in step and (dest, sub) not in dests[i]
            ]
            free.sort(key=lambda i: ((source, sub) in dests[i]) == (sub > 0))
            if not free:
                rounds.append({})
                free = [len(rounds) - 1]
            rounds[free[0]][source, sub] = (row, dest, slot)
    return rounds


def on_device(queries, stretch_keys, stretch_values, cache_keys, cache_values, doc_lengths):
    n_ctx = lax.axis_size("ctx")
    n_sub = lax.axis_size("sub")
    ctx_pos = lax.axis_index("ctx")
    sub_pos = lax.axis_index("sub")
    tok_rows = queries.shape[0]
    stretch_part, all_cols = stretch_keys.shape
    cache_part = cache_keys.shape[0]
    prefix_len = cache_part * n_sub * n_ctx
    head_cols = queries.shape[1] // n_sub
    reach = n_ctx // 2
    assert cache_part == 3 * stretch_part and tok_rows == 2 * stretch_part
    kv_cols = all_cols // n_sub if all_cols // HEAD_DIM % n_sub == 0 else all_cols
    vmem = pl.BlockSpec(memory_space=pltpu.VMEM)
    hbm = pl.BlockSpec(memory_space=pltpu.HBM)
    small = pltpu.CompilerParams(vmem_limit_bytes=8 << 20)

    def in_hbm(*arrays):
        return [pltpu.with_memory_space_constraint(x, pltpu.HBM) for x in arrays]

    rounds = plan_rounds(n_ctx, n_sub, reach, tok_rows, cache_part, cache_part * n_sub)
    owners = {
        (source, row // cache_part)
        for step in rounds
        for (source, _), (first, _, _) in step.items()
        if first is not None
        for row in (first, first + tok_rows - 1)
    }
    half = jax.ShapeDtypeStruct((stretch_part + cache_part, 2 * kv_cols), stretch_keys.dtype)
    raw, mine, theirs = pl.pallas_call(
        functools.partial(pack_kernel, n_ctx, sorted(owners)),
        out_shape=[
            jax.ShapeDtypeStruct((stretch_part, 2 * all_cols), stretch_keys.dtype), half, half
        ],
        in_specs=[hbm] * 4,
        out_specs=[vmem] * 3,
        scratch_shapes=[pltpu.SemaphoreType.DMA((3,))],
        compiler_params=small,
    )(*in_hbm(stretch_keys, stretch_values, cache_keys, cache_values))
    bias = pl.pallas_call(
        functools.partial(bias_kernel, prefix_len, stretch_part, cache_part),
        out_shape=jax.ShapeDtypeStruct((tok_rows, (reach + 1) * tok_rows), jnp.float32),
        in_specs=[hbm],
        out_specs=vmem,
        scratch_shapes=[pltpu.SMEM(doc_lengths.shape, jnp.int32), pltpu.SemaphoreType.DMA],
        compiler_params=small,
    )(*in_hbm(doc_lengths))

    peers = swap_cores(theirs)
    near = lax.ppermute(raw, "ctx", [(i, (i + 1) % n_ctx) for i in range(n_ctx)])

    def cached_rows(row):
        parts = []
        for owner in range(n_sub):
            low = max(row, owner * cache_part) - owner * cache_part + stretch_part
            high = min(row + tok_rows, (owner + 1) * cache_part) - owner * cache_part + stretch_part
            if low < high:
                parts.append(jnp.where(sub_pos == owner, mine[low:high], peers[low:high]))
        return jnp.concatenate(parts) if len(parts) > 1 else parts[0]

    own = jnp.concatenate([mine[:stretch_part], peers[:stretch_part]])
    sent, later, picks = [], [], []
    for step in rounds:
        block = own
        for source, row in sorted({(src, leg[0]) for (src, _), leg in step.items() if leg[0] is not None}):
            block = jnp.where(ctx_pos == source, cached_rows(row), block)
        pairs = [(src * n_sub + sub, leg[1] * n_sub + sub) for (src, sub), leg in step.items()]
        sent.append(block)
        later.append(lax.ppermute(block, ("ctx", "sub"), pairs))
        picks.append([(dest, sub, slot) for (_, sub), (_, dest, slot) in step.items()])

    near, *_ = lax.optimization_barrier((near, *sent[::-1]))
    if kv_cols != all_cols:
        at = (1 - sub_pos) * kv_cols
        near_theirs = jnp.concatenate(
            [
                lax.dynamic_slice_in_dim(near, at, kv_cols, 1),
                lax.dynamic_slice_in_dim(near, at + all_cols, kv_cols, 1),
            ],
            axis=1,
        )
    else:
        near_theirs = near
    far = swap_cores(near_theirs)
    mine_q = lax.dynamic_slice_in_dim(queries, sub_pos * head_cols, head_cols, 1)
    state = jax.ShapeDtypeStruct((tok_rows, head_cols), jnp.float32)
    large = pltpu.CompilerParams(vmem_limit_bytes=24 << 20)
    row_max, row_sum, weighted = pl.pallas_call(
        near_kernel,
        out_shape=[state] * 3,
        in_specs=[vmem] * 6,
        out_specs=[vmem] * 3,
        compiler_params=large,
    )(mine_q, bias, mine, peers, near, far)
    return pl.pallas_call(
        functools.partial(later_kernel, picks),
        out_shape=jax.ShapeDtypeStruct((tok_rows, head_cols), queries.dtype),
        in_specs=[vmem] * (5 + len(later)),
        out_specs=hbm,
        scratch_shapes=[
            pltpu.VMEM((tok_rows, head_cols), queries.dtype),
            pltpu.SemaphoreType.DMA,
        ],
        compiler_params=large,
    )(mine_q, bias, row_max, row_sum, weighted, *later)


def solution(mesh):
    in_specs = (
        P(("grp", "ctx"), "head"),
        P(("grp", "ctx", "sub"), "head"),
        P(("grp", "ctx", "sub"), "head"),
        P(("grp", "ctx", "sub"), "head"),
        P(("grp", "ctx", "sub"), "head"),
        P("grp"),
    )
    out_specs = P(("grp", "ctx"), ("head", "sub"))
    return jax.shard_map(
        on_device, mesh=mesh, in_specs=in_specs, out_specs=out_specs, check_vma=False
    )
```
